256 devices in a mesh: section: 4 (over x), row: 4 (over y), col: 16 (over z, core).
Axes of the slice: x: 4, y: 4, z: 8, core: 2. Of those that a mesh axis runs over, the one named last changes fastest.
Arguments:
- hidden_in: bfloat16 [2, 256, 8192], P(None, None, 'col'), may hold values from -24 to 24
- lengths: int32 [2, 32], replicated, may hold values from 1 to 64, 256 in all within a row
- gain: float32 [4, 8192], P('section', 'col'), may hold values from 0.1 to 1.9
- w_query: bfloat16 [4, 8192, 8192], P('section', 'col', 'row'), may hold values from -0.09375 to 0.09375
- w_pair: bfloat16 [4, 8192, 2048], P('section', 'col', 'row'), may hold values from -0.0625 to 0.0625
- w_out: bfloat16 [4, 8192, 8192], P('section', 'row', 'col'), may hold values from -0.0625 to 0.0625
Outputs:
- hidden_states: bfloat16 [4, 2, 256, 8192], P('section', None, None, 'col')
The draws below stay inside these ranges and needn't reach their ends.
Inputs may be any that keep to these rules, and one draw needn't show every extreme that they name: Each row of lengths sums to 256, and its largest entry is exactly 64.
All inputs are finite; a program needn't handle non-finite values.
Results may differ from the reference program's by a relative error of at most 0.019.
Values may be sent and summed in bfloat16 or wider, within the bound.
No kernel may reach another device: no remote copies, remote signals or barrier semaphores. Data moves between devices by JAX's collectives and lax.ppermute only.
A program may use at most 64 MiB of HBM per device.

```python
import math
import jax
import jax.numpy as jnp
import numpy as np
from jax import lax

D = 8192
HEADS = 64
KV_HEADS = 8
HEAD = 128
TOK = 256
MICRO = 2
LAYERS = 4
NSEG = 32
MOST = 64


def draw_hidden_in(key, part):
    key = jax.random.fold_in(key, 11)
    key_base, key_lift = jax.random.split(key)
    feature = jnp.arange(D, dtype=jnp.float32) / D
    base = jax.random.truncated_normal(key_base, -4.0, 4.0, (MICRO, TOK, D), jnp.float32)
    column = jnp.power(10.0, feature - 0.5)
    lift = jax.random.uniform(key_lift, (MICRO, TOK, 1), jnp.float32, -0.5, 0.5)
    return (0.5 * base * column[None, None, :] * jnp.power(10.0, lift)).astype(jnp.bfloat16)


def strengthened(values, own_key, source, target, shards_of, factor):
    owner, partner = [(jnp.arange(values.shape[dim]) // (values.shape[dim] // shards_of)).reshape([-1 if axis == dim else 1 for axis in range(values.ndim)]) for dim in (source, target)]
    chosen = jax.random.permutation(own_key, shards_of)[partner]
    strong = (owner == chosen) | (owner == (partner + shards_of // 2) % shards_of)
    return jnp.where(strong, factor * values, values)


def shard_levels(key, dims, shards, least, largest):
    factor_of = 1.0
    for position, parts in shards:
        heights = jax.random.uniform(jax.random.fold_in(jax.random.fold_in(key, 6), position), (parts,), jnp.float32, least / len(shards), largest / len(shards))
        factor_of = factor_of * jnp.repeat(jnp.exp(heights), dims[position] // parts).reshape((-1,) + (1,) * (len(dims) - 1 - position))
    return factor_of


def length_profile(number_of, total, most, slope):
    weights = [(1 << 20) // math.isqrt(rank ** slope) + 1 for rank in range(2, number_of + 1)]
    spare, counts = total - most - (number_of - 1), [1] * (number_of - 1)
    while spare > 0:
        movable = [i for i in range(number_of - 1) if counts[i] < most]
        whole, left = sum([weights[i] for i in movable]), spare
        for i in movable:
            extra = min(most - counts[i], max(1, left * weights[i] // whole), spare)
            counts[i] = counts[i] + extra
            spare = spare - extra
    return np.array([most] + counts)


def ragged_sizes(own_key, count, total, reach, skew):
    if count == 2:
        one = jax.random.randint(own_key, (), max(1, total - reach), min(reach, total - 1) + 1)
        return jnp.stack([one, total - one])
    tallies = jnp.asarray(length_profile(count, total, reach, skew), jnp.int32)
    couples = (count - 1) // 2
    source_of, sink = tallies[1:1 + 2 * couples:2], tallies[2:2 + 2 * couples:2]
    slack = jnp.minimum(source_of - 1, reach - sink)
    shifted = jax.random.randint(jax.random.fold_in(own_key, 1), (couples,), 0, 1 << 20) % (slack + 1)
    tallies = tallies.at[1:1 + 2 * couples:2].set(source_of - shifted).at[2:2 + 2 * couples:2].set(sink + shifted)
    return tallies[jax.random.permutation(jax.random.fold_in(own_key, 2), count)]


def centred(rng, extent, width, limit, cuts=(), kind=jnp.bfloat16):
    array = jax.random.normal(rng, extent, jnp.float32) * width
    if len(cuts) > 0:
        array = shard_levels(rng, extent, cuts, -0.22, 0.18) * array
    return jnp.clip(array, min=-limit, max=limit).astype(kind)


def noise_with(rng, extent, spread, bound, cuts, heavy, held_as=jnp.bfloat16):
    array = spread * jax.random.normal(rng, extent, jnp.float32)
    if cuts:
        array = array * shard_levels(rng, extent, cuts, -0.22, 0.18)
    return jnp.clip(strengthened(array, jax.random.fold_in(rng, 3), *heavy), -bound, bound).astype(held_as)


def setup_inputs(seed: int = 0) -> dict:
    seeds = jax.random.split(jax.random.key(seed), 7)
    return {
        "hidden_in": draw_hidden_in(jax.random.fold_in(seeds[6], 71), 0),
        "lengths": jax.vmap(lambda own: ragged_sizes(own, NSEG, TOK, MOST, 2))(jax.random.split(seeds[1], MICRO)).reshape((MICRO, NSEG)).astype(jnp.int32),
        "gain": jnp.clip(1.0 + 0.18 * jax.random.normal(seeds[2], (LAYERS, D), jnp.float32), 0.1, 1.9),
        "w_query": noise_with(seeds[3], (LAYERS, D, HEADS * HEAD), D ** -0.5, 0.09375, ((0, 4), (1, 16), (2, 4)), (1, 2, 16, 2.0)),
        "w_pair": centred(seeds[4], (LAYERS, D, KV_HEADS * 2 * HEAD), D ** -0.5, 0.0625, ((0, 4), (1, 16), (2, 4))),
        "w_out": centred(seeds[5], (LAYERS, HEADS * HEAD, D), (HEADS * HEAD) ** -0.5, 0.0625, ((0, 4), (1, 4), (2, 16))),
    }


ROPE_BASE = 500000.0
EPSILON = 1e-05

def segment_info(lengths_row, total):
    token_ids = jnp.arange(total, dtype=jnp.int32)
    ends = jnp.cumsum(lengths_row).astype(jnp.int32)
    after = (token_ids[:, None] >= ends[None, :]).astype(jnp.int32)
    seg_ids = lax.optimization_barrier(jnp.sum(after, axis=1)).astype(jnp.int32)
    starts = lax.optimization_barrier(jnp.sum(after * lengths_row[None, :], axis=1)).astype(jnp.int32)
    return (seg_ids, (token_ids - starts).astype(jnp.int32))

def rotate(values, positions):
    half = values.shape[-1] // 2
    exponent = jnp.arange(half, dtype=jnp.float32) * (2.0 / values.shape[-1])
    freqs = jnp.power(jnp.float32(ROPE_BASE), -exponent)
    angles = positions.astype(jnp.float32)[:, None] * freqs[None, :]
    cosine = jnp.cos(angles)[:, None, :]
    sine = jnp.sin(angles)[:, None, :]
    first = values[..., :half]
    second = values[..., half:]
    return jnp.concatenate([first * cosine - second * sine, second * cosine + first * sine], axis=-1)

def layer_step(hidden, seg_ids, positions, gain_row, query_w, pair_w, out_w):
    wide = hidden.astype(jnp.float32)
    scaled = (wide * gain_row.astype(jnp.float32)[None, :]).astype(jnp.bfloat16)
    inverse = lax.rsqrt(lax.optimization_barrier(jnp.sum(wide * wide, axis=1)) / D + EPSILON)
    query_full = jnp.dot(scaled, query_w, preferred_element_type=jnp.float32) * inverse[:, None]
    pair_full = jnp.dot(scaled, pair_w, preferred_element_type=jnp.float32) * inverse[:, None]
    queries = rotate(query_full.reshape(TOK, HEADS, HEAD), positions).astype(jnp.bfloat16)
    pairs = pair_full.reshape(TOK, KV_HEADS, 2, HEAD)
    keys = rotate(pairs[:, :, 0], positions).astype(jnp.bfloat16)
    values = pairs[:, :, 1].astype(jnp.bfloat16)
    grouped = queries.reshape(TOK, KV_HEADS, HEADS // KV_HEADS, HEAD).astype(jnp.float32)
    scores = jnp.einsum('qhgd,khd->hgqk', grouped, keys.astype(jnp.float32)) * HEAD ** (-0.5)
    allowed = (seg_ids[:, None] == seg_ids[None, :]) & (positions[None, :] <= positions[:, None])
    raised = jnp.where(allowed[None, None], jnp.exp(scores), jnp.float32(0.0))
    weights = (raised / lax.optimization_barrier(jnp.sum(raised, axis=-1, keepdims=True))).astype(jnp.bfloat16)
    mixed = jnp.einsum('hgqk,khd->qhgd', weights.astype(jnp.float32), values.astype(jnp.float32))
    mixed = mixed.astype(jnp.bfloat16).reshape(TOK, HEADS * HEAD)
    branch = jnp.dot(mixed, out_w, preferred_element_type=jnp.float32)
    return (wide + branch).astype(jnp.bfloat16)

def reference(hidden_in, lengths, gain, w_query, w_pair, w_out):

    def one_micro(entry):
        hidden, lengths_row = entry
        seg_ids, positions = segment_info(lengths_row, TOK)
        states = []
        for layer in range(w_query.shape[0]):
            hidden = layer_step(hidden, seg_ids, positions, gain[layer], w_query[layer], w_pair[layer], w_out[layer])
            states.append(hidden)
        return jnp.stack(states)
    stacked = lax.map(one_micro, (hidden_in, lengths))
    return jnp.transpose(stacked, (1, 0, 2, 3))
```

```python
import jax
import jax.numpy as jnp
from jax import lax
from jax.experimental import pallas as pl
from jax.experimental.pallas import tpu as pltpu
from jax.sharding import Mesh
from jax.sharding import PartitionSpec as P

HEAD = 128
WIDTH = 8192
TOK = 256
LAYERS = 4
ROPE_BASE = 500000.0
EPSILON = 1e-05

CHIPS = 8
OWN = TOK // CHIPS
HALO = 64
WINDOW = HALO + OWN
PACK = 2 * OWN + WINDOW
GRID = 16
PART = TOK // GRID

bf16 = jnp.bfloat16
f32 = jnp.float32
VMEM = pl.BlockSpec(memory_space=pltpu.VMEM)
PARAMS = pltpu.CompilerParams(vmem_limit_bytes=40 * 1024 * 1024)


def call(kernel, outs, args, flops):
    nbytes = sum(a.size * a.dtype.itemsize for a in args)
    return pl.pallas_call(
        kernel,
        out_shape=outs,
        in_specs=[VMEM] * len(args),
        out_specs=jax.tree.map(lambda _: VMEM, outs),
        compiler_params=PARAMS,
        cost_estimate=pl.CostEstimate(flops=flops, bytes_accessed=nbytes, transcendentals=0),
    )(*args)


def project_kernel(x_ref, near_ref, far_ref, out_ref):
    x = x_ref[...]
    half = x.shape[1] // 2
    y = jnp.dot(x[:, :half], near_ref[...], preferred_element_type=f32)
    y = y + jnp.dot(x[:, half:], far_ref[...], preferred_element_type=f32)
    gram = lax.dot_general(x, x, (((1,), (1,)), ((), ())), preferred_element_type=f32)
    rows = lax.broadcasted_iota(jnp.int32, gram.shape, 0)
    cols = lax.broadcasted_iota(jnp.int32, gram.shape, 1)
    squares = jnp.sum(jnp.where(rows == cols, gram, 0.0), axis=0, keepdims=True)
    first = lax.broadcasted_iota(jnp.int32, (16, TOK), 0) == 0
    kv = y[:, 512:768]
    zero = jnp.zeros((16, TOK), f32)
    for d in range(CHIPS):
        own = slice(OWN * d, OWN * (d + 1))
        out_ref[d, 0:OWN, :] = y[own, 0:256].astype(bf16)
        out_ref[d, OWN : 2 * OWN, :] = y[own, 256:512].astype(bf16)
        begin = OWN * d - HALO
        for r in range(0, WINDOW, 16):
            t = begin + r
            block = kv[t : t + 16] if t >= 0 else zero
            if r == 0:
                block = jnp.where(first, squares, block)
            out_ref[d, 2 * OWN + r : 2 * OWN + r + 16, :] = block.astype(bf16)


def attend_kernel(place_ref, recv_ref, cos_ref, sin_ref, mask_ref, out_ref):
    total = recv_ref[0].astype(f32)
    for d in range(1, CHIPS):
        total = total + recv_ref[d].astype(f32)
    squares = total[2 * OWN : 2 * OWN + 1, :]
    inverse_row = lax.rsqrt(squares * (1.0 / WIDTH) + EPSILON)
    token = lax.broadcasted_iota(jnp.int32, (WINDOW, TOK), 0) + (place_ref[0] * OWN - HALO)
    lane = lax.broadcasted_iota(jnp.int32, (WINDOW, TOK), 1)
    inverse = jnp.sum(jnp.where(token == lane, inverse_row, 0.0), axis=1, keepdims=True)
    cosine = cos_ref[...]
    sine = sin_ref[...]

    def rope(v, c, s):
        return (v * c + pltpu.roll(v, HEAD // 2, 1) * s).astype(bf16)

    scaled = total[2 * OWN :, :] * inverse
    keys = rope(scaled[:, :HEAD], cosine, sine)
    values = scaled[:, HEAD:].astype(bf16)
    own_inverse = inverse[HALO:]
    queries = []
    for h in range(4):
        rows = slice((h // 2) * OWN, (h // 2 + 1) * OWN)
        lanes = slice((h % 2) * HEAD, (h % 2 + 1) * HEAD)
        queries.append(rope(total[rows, lanes] * own_inverse, cosine[HALO:], sine[HALO:]))
    queries = jnp.concatenate(queries, axis=0)
    scores = lax.dot_general(queries, keys, (((1,), (1,)), ((), ())), preferred_element_type=f32)
    raised = jnp.where(mask_ref[...] > 0.0, jnp.exp(scores * (HEAD**-0.5)), 0.0)
    weights = (raised / jnp.sum(raised, axis=1, keepdims=True)).astype(bf16)
    mixed = jnp.dot(weights, values, preferred_element_type=f32).astype(bf16)
    for d in range(CHIPS):
        for h in range(4):
            out_ref[d, :, h * HEAD : (h + 1) * HEAD] = mixed[h * OWN : (h + 1) * OWN]


def out_kernel(mixed_ref, near_ref, far_ref, out_ref):
    mixed = mixed_ref[...]
    half = near_ref.shape[1]
    out_ref[:, :half] = jnp.dot(mixed, near_ref[...], preferred_element_type=f32).astype(bf16)
    out_ref[:, half:] = jnp.dot(mixed, far_ref[...], preferred_element_type=f32).astype(bf16)


def sum_kernel(recv_ref, held_ref, out_ref, own_ref):
    total = held_ref[...].astype(f32)
    for d in range(GRID):
        total = total + recv_ref[d].astype(f32)
    own = total.astype(bf16)
    own_ref[...] = own
    for d in range(GRID):
        out_ref[d] = own


def segment_info(lengths_row, total):
    token_ids = jnp.arange(total, dtype=jnp.int32)
    ends = jnp.cumsum(lengths_row)
    after = (token_ids[:, None] >= ends[None, :]).astype(jnp.int32)
    seg_ids = jnp.sum(after, axis=1)
    starts = jnp.sum(after * lengths_row[None, :], axis=1)
    return (seg_ids, token_ids - starts)


def swap(value):
    return lax.ppermute(value, "core", [(0, 1), (1, 0)])


def exchange(value, axis):
    return lax.all_to_all(value, axis, 0, 0, tiled=True)


def local(hidden_in, lengths, gain, w_query, w_pair, w_out):
    section = lax.axis_index("section")
    place = lax.axis_index("z")
    core = lax.axis_index("core")
    grid_place = section * 4 + lax.axis_index("row")

    queries_w = w_query[0].reshape(512, 4, 512).transpose(1, 0, 2)
    pairs_w = jnp.repeat(w_pair[0].reshape(512, 2, 256).transpose(1, 0, 2), 2, axis=0)
    send_in = jnp.concatenate([queries_w, pairs_w], axis=2).astype(f32) * gain[0][None, :, None]
    near_in = exchange(send_in.astype(bf16), "section")
    far_in = swap(near_in)
    near_out = exchange(w_out[0].reshape(4, 512, 512), "section")
    far_out = swap(near_out)

    mine = lax.dynamic_index_in_dim(hidden_in, core, 0, keepdims=False)
    theirs = lax.dynamic_index_in_dim(hidden_in, 1 - core, 0, keepdims=False)
    x = jnp.concatenate([mine, swap(theirs)], axis=1)
    held = lax.dynamic_slice_in_dim(x, grid_place * PART, PART, 0)

    seg, pos = segment_info(lax.dynamic_index_in_dim(lengths, core, 0, keepdims=False), TOK)
    seg_window = lax.dynamic_slice_in_dim(jnp.pad(seg, (HALO, 0), constant_values=-1), place * OWN, WINDOW)
    pos_window = lax.dynamic_slice_in_dim(jnp.pad(pos, (HALO, 0)), place * OWN, WINDOW)
    exponent = jnp.arange(HEAD // 2, dtype=f32) * (2.0 / HEAD)
    freqs = jnp.power(f32(ROPE_BASE), -exponent)
    angles = pos_window.astype(f32)[:, None] * freqs[None, :]
    cosine = jnp.cos(angles)
    sine = jnp.sin(angles)
    cosine = jnp.concatenate([cosine, cosine], axis=1)
    sine = jnp.concatenate([-sine, sine], axis=1)
    allowed = (seg_window[HALO:, None] == seg_window[None, :]) & (pos_window[None, :] <= pos_window[HALO:, None])
    mask = jnp.tile(allowed.astype(f32), (4, 1))
    place_arg = place.reshape(1).astype(jnp.int32)

    def attend(recv):
        return pl.pallas_call(
            attend_kernel,
            out_shape=jax.ShapeDtypeStruct((CHIPS, OWN, 512), bf16),
            in_specs=[pl.BlockSpec(memory_space=pltpu.SMEM)] + [VMEM] * 4,
            out_specs=VMEM,
            compiler_params=PARAMS,
            cost_estimate=pl.CostEstimate(flops=10_000_000, bytes_accessed=1_000_000, transcendentals=20_000),
        )(place_arg, recv, cosine, sine, mask)

    states = []
    for layer in range(LAYERS):
        packed = call(
            project_kernel,
            jax.ShapeDtypeStruct((CHIPS, PACK, 256), bf16),
            (x, near_in[layer], far_in[layer]),
            2 * 256 * 1024 * 1024,
        )
        mixed = exchange(attend(exchange(packed, "z")), "z").reshape(TOK, 512)
        branch = call(
            out_kernel,
            jax.ShapeDtypeStruct((TOK, 1024), bf16),
            (mixed, near_out[layer], far_out[layer]),
            2 * 256 * 512 * 1024,
        )
        copies, held = call(
            sum_kernel,
            (jax.ShapeDtypeStruct((GRID, PART, 1024), bf16), jax.ShapeDtypeStruct((PART, 1024), bf16)),
            (exchange(branch.reshape(GRID, PART, 1024), ("section", "row")), held),
            256 * 1024,
        )
        x = exchange(copies, ("section", "row")).reshape(TOK, 1024)
        states.append(x)

    kept = states[0]
    for layer in range(1, LAYERS):
        kept = jnp.where(section == layer, states[layer], kept)
    ours = kept[:, :512]
    other = swap(kept[:, 512:])
    final = jnp.where(core == 0, jnp.stack([ours, other]), jnp.stack([other, ours]))
    return final[None]


def solution(mesh):
    split = Mesh(mesh.devices.reshape(4, 4, 8, 2), ("section", "row", "z", "core"))
    col = ("z", "core")
    in_specs = (
        P(None, None, col),
        P(),
        P("section", col),
        P("section", col, "row"),
        P("section", col, "row"),
        P("section", "row", col),
    )
    out_specs = P("section", None, None, col)
    return jax.shard_map(local, mesh=split, in_specs=in_specs, out_specs=out_specs, check_vma=False)
```

```python
import jax
import jax.numpy as jnp
from jax import lax
from jax.experimental import pallas as pl
from jax.experimental.pallas import tpu as pltpu
from jax.sharding import Mesh
from jax.sharding import PartitionSpec as P

HEAD = 128
WIDTH = 8192
TOK = 256
LAYERS = 4
ROPE_BASE = 500000.0
EPSILON = 1e-05

CHIPS = 8
OWN = TOK // CHIPS
HALO = 64
WINDOW = HALO + OWN
PACK = 2 * OWN + WINDOW
GRID = 16
PART = TOK // GRID

bf16 = jnp.bfloat16
f32 = jnp.float32
VMEM = pl.BlockSpec(memory_space=pltpu.VMEM)
PARAMS = pltpu.CompilerParams(vmem_limit_bytes=40 * 1024 * 1024)


def call(kernel, outs, args, flops):
    nbytes = sum(a.size * a.dtype.itemsize for a in args)
    return pl.pallas_call(
        kernel,
        out_shape=outs,
        in_specs=[VMEM] * len(args),
        out_specs=jax.tree.map(lambda _: VMEM, outs),
        compiler_params=PARAMS,
        cost_estimate=pl.CostEstimate(flops=flops, bytes_accessed=nbytes, transcendentals=0),
    )(*args)


def project_kernel(x_ref, near_ref, far_ref, out_ref):
    x = x_ref[...]
    half = x.shape[1] // 2
    y = jnp.dot(x[:, :half], near_ref[...], preferred_element_type=f32)
    y = y + jnp.dot(x[:, half:], far_ref[...], preferred_element_type=f32)
    gram = lax.dot_general(x, x, (((1,), (1,)), ((), ())), preferred_element_type=f32)
    rows = lax.broadcasted_iota(jnp.int32, gram.shape, 0)
    cols = lax.broadcasted_iota(jnp.int32, gram.shape, 1)
    squares = jnp.sum(jnp.where(rows == cols, gram, 0.0), axis=0, keepdims=True)
    first = lax.broadcasted_iota(jnp.int32, (16, TOK), 0) == 0
    kv = y[:, 512:768]
    zero = jnp.zeros((16, TOK), f32)
    for d in range(CHIPS):
        own = slice(OWN * d, OWN * (d + 1))
        out_ref[d, 0:OWN, :] = y[own, 0:256].astype(bf16)
        out_ref[d, OWN : 2 * OWN, :] = y[own, 256:512].astype(bf16)
        begin = OWN * d - HALO
        for r in range(0, WINDOW, 16):
            t = begin + r
            block = kv[t : t + 16] if t >= 0 else zero
            if r == 0:
                block = jnp.where(first, squares, block)
            out_ref[d, 2 * OWN + r : 2 * OWN + r + 16, :] = block.astype(bf16)


def attend_kernel(place_ref, recv_ref, cos_ref, sin_ref, mask_ref, out_ref):
    total = recv_ref[0].astype(f32)
    for d in range(1, CHIPS):
        total = total + recv_ref[d].astype(f32)
    squares = total[2 * OWN : 2 * OWN + 1, :]
    inverse_row = lax.rsqrt(squares * (1.0 / WIDTH) + EPSILON)
    token = lax.broadcasted_iota(jnp.int32, (WINDOW, TOK), 0) + (place_ref[0] * OWN - HALO)
    lane = lax.broadcasted_iota(jnp.int32, (WINDOW, TOK), 1)
    inverse = jnp.sum(jnp.where(token == lane, inverse_row, 0.0), axis=1, keepdims=True)
    cosine = cos_ref[...]
    sine = sin_ref[...]

    def rope(v, c, s):
        return (v * c + pltpu.roll(v, HEAD // 2, 1) * s).astype(bf16)

    scaled = total[2 * OWN :, :] * inverse
    keys = rope(scaled[:, :HEAD], cosine, sine)
    values = scaled[:, HEAD:].astype(bf16)
    own_inverse = inverse[HALO:]
    queries = []
    for h in range(4):
        rows = slice((h // 2) * OWN, (h // 2 + 1) * OWN)
        lanes = slice((h % 2) * HEAD, (h % 2 + 1) * HEAD)
        queries.append(rope(total[rows, lanes] * own_inverse, cosine[HALO:], sine[HALO:]))
    queries = jnp.concatenate(queries, axis=0)
    scores = lax.dot_general(queries, keys, (((1,), (1,)), ((), ())), preferred_element_type=f32)
    raised = jnp.where(mask_ref[...] > 0.0, jnp.exp(scores * (HEAD**-0.5)), 0.0)
    weights = (raised / jnp.sum(raised, axis=1, keepdims=True)).astype(bf16)
    mixed = jnp.dot(weights, values, preferred_element_type=f32).astype(bf16)
    for d in range(CHIPS):
        for h in range(4):
            out_ref[d, :, h * HEAD : (h + 1) * HEAD] = mixed[h * OWN : (h + 1) * OWN]


def out_kernel(mixed_ref, near_ref, far_ref, out_ref):
    mixed = mixed_ref[...]
    half = near_ref.shape[1]
    out_ref[:, :half] = jnp.dot(mixed, near_ref[...], preferred_element_type=f32).astype(bf16)
    out_ref[:, half:] = jnp.dot(mixed, far_ref[...], preferred_element_type=f32).astype(bf16)


def sum_kernel(recv_ref, held_ref, out_ref, own_ref):
    total = held_ref[...].astype(f32)
    for d in range(GRID):
        total = total + recv_ref[d].astype(f32)
    own = total.astype(bf16)
    own_ref[...] = own
    for d in range(GRID):
        out_ref[d] = own


def weigh_kernel(dest_ref, query_ref, pair_ref, gain_ref, out_ref):
    rows = lax.broadcasted_iota(jnp.int32, (128, 128), 0)
    cols = lax.broadcasted_iota(jnp.int32, (128, 128), 1)
    scale = jnp.sum(jnp.where(rows == cols, gain_ref[...], 0.0), axis=1, keepdims=True)
    out_ref[:, :512] = (query_ref[0].astype(f32) * scale).astype(bf16)
    out_ref[:, 512:] = (pair_ref[0].astype(f32) * scale).astype(bf16)


def weigh(w_query, w_pair, gain, dest):
    return pl.pallas_call(
        weigh_kernel,
        out_shape=jax.ShapeDtypeStruct((512, 768), bf16),
        grid_spec=pltpu.PrefetchScalarGridSpec(
            num_scalar_prefetch=1,
            grid=(4,),
            in_specs=[
                pl.BlockSpec((1, 128, 512), lambda i, d: (0, i, d[0])),
                pl.BlockSpec((1, 128, 256), lambda i, d: (0, i, d[0] // 2)),
                pl.BlockSpec((1, 128), lambda i, d: (0, i)),
            ],
            out_specs=pl.BlockSpec((128, 768), lambda i, d: (i, 0)),
        ),
        compiler_params=PARAMS,
        cost_estimate=pl.CostEstimate(flops=1_000_000, bytes_accessed=1_600_000, transcendentals=0),
    )(dest.reshape(1).astype(jnp.int32), w_query, w_pair, gain)


def pick_kernel(index_ref, *refs):
    *sources, out_ref, sem = refs
    for i, source in enumerate(sources):

        @pl.when(index_ref[0] == i)
        def _():
            copy = pltpu.make_async_copy(source, out_ref, sem)
            copy.start()
            copy.wait()


def pick(arrays, index):
    return pl.pallas_call(
        pick_kernel,
        out_shape=jax.ShapeDtypeStruct(arrays[0].shape, arrays[0].dtype),
        in_specs=[pl.BlockSpec(memory_space=pltpu.SMEM)] + [pl.BlockSpec(memory_space=pl.ANY)] * len(arrays),
        out_specs=pl.BlockSpec(memory_space=pl.ANY),
        scratch_shapes=[pltpu.SemaphoreType.DMA],
        compiler_params=PARAMS,
        cost_estimate=pl.CostEstimate(flops=0, bytes_accessed=1_500_000, transcendentals=0),
    )(index.reshape(1).astype(jnp.int32), *arrays)


def rotated(value, steps, first):
    return lax.ppermute(value, "section", [(s, (s + steps) % 4) for s in range(first, 4)])


def segment_info(lengths_row, total):
    token_ids = jnp.arange(total, dtype=jnp.int32)
    ends = jnp.cumsum(lengths_row)
    after = (token_ids[:, None] >= ends[None, :]).astype(jnp.int32)
    seg_ids = jnp.sum(after, axis=1)
    starts = jnp.sum(after * lengths_row[None, :], axis=1)
    return (seg_ids, token_ids - starts)


def swap(value):
    return lax.ppermute(value, "core", [(0, 1), (1, 0)])


def exchange(value, axis):
    return lax.all_to_all(value, axis, 0, 0, tiled=True)


def local(hidden_in, lengths, gain, w_query, w_pair, w_out):
    section = lax.axis_index("section")
    place = lax.axis_index("z")
    core = lax.axis_index("core")
    grid_place = section * 4 + lax.axis_index("row")

    blocks_in = [weigh(w_query, w_pair, gain, (section + k) % 4) for k in range(4)]
    blocks_out = [lax.dynamic_slice(w_out, (0, 512 * ((section + k) % 4), 0), (1, 512, 512))[0] for k in range(4)]
    first_in = [blocks_in[0]] + [lax.ppermute(blocks_in[k], "section", [(0, k)]) for k in range(1, 4)]
    near_in = pick(first_in, section)
    far_in = swap(near_in)
    turn = [(section - layer) % 4 for layer in range(LAYERS)]
    ready, *blocks_out = lax.optimization_barrier((near_in, *blocks_out))
    moved_out = [blocks_out[0]] + [rotated(blocks_out[k], k, 0) for k in range(1, 4)]

    mine = lax.dynamic_index_in_dim(hidden_in, core, 0, keepdims=False)
    theirs = lax.dynamic_index_in_dim(hidden_in, 1 - core, 0, keepdims=False)
    x = jnp.concatenate([mine, swap(theirs)], axis=1)
    held = lax.dynamic_slice_in_dim(x, grid_place * PART, PART, 0)

    seg, pos = segment_info(lax.dynamic_index_in_dim(lengths, core, 0, keepdims=False), TOK)
    seg_window = lax.dynamic_slice_in_dim(jnp.pad(seg, (HALO, 0), constant_values=-1), place * OWN, WINDOW)
    pos_window = lax.dynamic_slice_in_dim(jnp.pad(pos, (HALO, 0)), place * OWN, WINDOW)
    exponent = jnp.arange(HEAD // 2, dtype=f32) * (2.0 / HEAD)
    freqs = jnp.power(f32(ROPE_BASE), -exponent)
    angles = pos_window.astype(f32)[:, None] * freqs[None, :]
    cosine = jnp.cos(angles)
    sine = jnp.sin(angles)
    cosine = jnp.concatenate([cosine, cosine], axis=1)
    sine = jnp.concatenate([-sine, sine], axis=1)
    allowed = (seg_window[HALO:, None] == seg_window[None, :]) & (pos_window[None, :] <= pos_window[HALO:, None])
    mask = jnp.tile(allowed.astype(f32), (4, 1))
    place_arg = place.reshape(1).astype(jnp.int32)

    def attend(recv):
        return pl.pallas_call(
            attend_kernel,
            out_shape=jax.ShapeDtypeStruct((CHIPS, OWN, 512), bf16),
            in_specs=[pl.BlockSpec(memory_space=pltpu.SMEM)] + [VMEM] * 4,
            out_specs=VMEM,
            compiler_params=PARAMS,
            cost_estimate=pl.CostEstimate(flops=10_000_000, bytes_accessed=1_000_000, transcendentals=20_000),
        )(place_arg, recv, cosine, sine, mask)

    states = []
    for layer in range(LAYERS):
        if layer > 0:
            near_in = pick(moved_in, turn[layer])
            far_in = swap(near_in)
        packed = call(
            project_kernel,
            jax.ShapeDtypeStruct((CHIPS, PACK, 256), bf16),
            (x, near_in, far_in),
            2 * 256 * 1024 * 1024,
        )
        if layer == 0:
            packed, *blocks_in = lax.optimization_barrier((packed, *blocks_in))
            moved_in = [blocks_in[0]] + [rotated(blocks_in[k], k, 1) for k in range(1, 4)]
        near_out = pick(moved_out, turn[layer])
        far_out = swap(near_out)
        mixed = exchange(attend(exchange(packed, "z")), "z").reshape(TOK, 512)
        branch = call(
            out_kernel,
            jax.ShapeDtypeStruct((TOK, 1024), bf16),
            (mixed, near_out, far_out),
            2 * 256 * 512 * 1024,
        )
        copies, held = call(
            sum_kernel,
            (jax.ShapeDtypeStruct((GRID, PART, 1024), bf16), jax.ShapeDtypeStruct((PART, 1024), bf16)),
            (exchange(branch.reshape(GRID, PART, 1024), ("section", "row")), held),
            256 * 1024,
        )
        x = exchange(copies, ("section", "row")).reshape(TOK, 1024)
        states.append(x)

    kept = states[0]
    for layer in range(1, LAYERS):
        kept = jnp.where(section == layer, states[layer], kept)
    ours = kept[:, :512]
    other = swap(kept[:, 512:])
    final = jnp.where(core == 0, jnp.stack([ours, other]), jnp.stack([other, ours]))
    return final[None]


def solution(mesh):
    split = Mesh(mesh.devices.reshape(4, 4, 8, 2), ("section", "row", "z", "core"))
    col = ("z", "core")
    in_specs = (
        P(None, None, col),
        P(),
        P("section", col),
        P("section", col, "row"),
        P("section", col, "row"),
        P("section", "row", col),
    )
    out_specs = P("section", None, None, col)
    return jax.shard_map(local, mesh=split, in_specs=in_specs, out_specs=out_specs, check_vma=False)
```

```python
import jax
import jax.numpy as jnp
from jax import lax
from jax.experimental import pallas as pl
from jax.experimental.pallas import tpu as pltpu
from jax.sharding import Mesh
from jax.sharding import PartitionSpec as P

HEAD = 128
WIDTH = 8192
TOK = 256
LAYERS = 4
ROPE_BASE = 500000.0
EPSILON = 1e-05

CHIPS = 8
OWN = TOK // CHIPS
HALO = 64
WINDOW = HALO + OWN
PACK = 2 * OWN + WINDOW
GRID = 16
PART = TOK // GRID

bf16 = jnp.bfloat16
f32 = jnp.float32
VMEM = pl.BlockSpec(memory_space=pltpu.VMEM)
PARAMS = pltpu.CompilerParams(vmem_limit_bytes=12 * 1024 * 1024)
STREAM = pltpu.CompilerParams(vmem_limit_bytes=56 * 1024 * 1024)


def call(kernel, outs, args, flops):
    nbytes = sum(a.size * a.dtype.itemsize for a in args)
    return pl.pallas_call(
        kernel,
        out_shape=outs,
        in_specs=[VMEM] * len(args),
        out_specs=jax.tree.map(lambda _: VMEM, outs),
        compiler_params=PARAMS,
        cost_estimate=pl.CostEstimate(flops=flops, bytes_accessed=nbytes, transcendentals=0),
    )(*args)


def project(x, near, far, layer, far_layer, kept, flag):
    rows = 256
    outs = [jax.ShapeDtypeStruct((CHIPS, PACK, 256), bf16)]
    args = [x, near, far]
    in_specs = [
        VMEM,
        pl.BlockSpec((1, rows, 768), lambda i: (layer, i, 0)),
        pl.BlockSpec((1, rows, 768), lambda i: (far_layer, i, 0)),
    ]
    if kept is not None:
        outs.append(jax.ShapeDtypeStruct(kept.shape, bf16))
        args += [kept, flag]
        in_specs += [VMEM, pl.BlockSpec(memory_space=pltpu.SMEM)]
    return pl.pallas_call(
        project_kernel if kept is not None else first_project_kernel,
        out_shape=outs,
        grid=(2,),
        in_specs=in_specs,
        out_specs=[VMEM] * len(outs),
        scratch_shapes=[pltpu.VMEM((TOK, 768), f32)],
        compiler_params=PARAMS,
        cost_estimate=pl.CostEstimate(flops=2 * 256 * 1024 * 1024, bytes_accessed=3_000_000, transcendentals=0),
    )(*args)


def first_project_kernel(x_ref, near_ref, far_ref, out_ref, sum_ref):
    project_step(x_ref, near_ref, far_ref, out_ref, sum_ref)


def project_kernel(x_ref, near_ref, far_ref, kept_ref, flag_ref, out_ref, next_ref, sum_ref):
    project_step(x_ref, near_ref, far_ref, out_ref, sum_ref)

    @pl.when(pl.program_id(0) == 0)
    def _():
        next_ref[...] = jnp.where(flag_ref[0] == 1, x_ref[...], kept_ref[...])


def project_step(x_ref, near_ref, far_ref, out_ref, sum_ref):
    step = pl.program_id(0)
    near_x = x_ref[:, pl.ds(pl.multiple_of(step * 256, 256), 256)]
    far_x = x_ref[:, pl.ds(pl.multiple_of(512 + step * 256, 256), 256)]
    part = jnp.dot(near_x, near_ref[0], preferred_element_type=f32)
    part = part + jnp.dot(far_x, far_ref[0], preferred_element_type=f32)

    @pl.when(step == 0)
    def _():
        sum_ref[...] = part

    @pl.when(step == 1)
    def _():
        pack(x_ref[...], sum_ref[...] + part, out_ref)


def pack(x, y, out_ref):
    gram = lax.dot_general(x, x, (((1,), (1,)), ((), ())), preferred_element_type=f32)
    rows = lax.broadcasted_iota(jnp.int32, gram.shape, 0)
    cols = lax.broadcasted_iota(jnp.int32, gram.shape, 1)
    squares = jnp.sum(jnp.where(rows == cols, gram, 0.0), axis=0, keepdims=True)
    first = lax.broadcasted_iota(jnp.int32, (16, TOK), 0) == 0
    kv = y[:, 512:768]
    zero = jnp.zeros((16, TOK), f32)
    for d in range(CHIPS):
        own = slice(OWN * d, OWN * (d + 1))
        out_ref[d, 0:OWN, :] = y[own, 0:256].astype(bf16)
        out_ref[d, OWN : 2 * OWN, :] = y[own, 256:512].astype(bf16)
        begin = OWN * d - HALO
        for r in range(0, WINDOW, 16):
            t = begin + r
            block = kv[t : t + 16] if t >= 0 else zero
            if r == 0:
                block = jnp.where(first, squares, block)
            out_ref[d, 2 * OWN + r : 2 * OWN + r + 16, :] = block.astype(bf16)


def attend_kernel(place_ref, recv_ref, cos_ref, sin_ref, mask_ref, out_ref):
    total = recv_ref[0].astype(f32)
    for d in range(1, CHIPS):
        total = total + recv_ref[d].astype(f32)
    squares = total[2 * OWN : 2 * OWN + 1, :]
    inverse_row = lax.rsqrt(squares * (1.0 / WIDTH) + EPSILON)
    token = lax.broadcasted_iota(jnp.int32, (WINDOW, TOK), 0) + (place_ref[0] * OWN - HALO)
    lane = lax.broadcasted_iota(jnp.int32, (WINDOW, TOK), 1)
    inverse = jnp.sum(jnp.where(token == lane, inverse_row, 0.0), axis=1, keepdims=True)
    cosine = cos_ref[...]
    sine = sin_ref[...]

    def rope(v, c, s):
        return (v * c + pltpu.roll(v, HEAD // 2, 1) * s).astype(bf16)

    scaled = total[2 * OWN :, :] * inverse
    keys = rope(scaled[:, :HEAD], cosine, sine)
    values = scaled[:, HEAD:].astype(bf16)
    own_inverse = inverse[HALO:]
    queries = []
    for h in range(4):
        rows = slice((h // 2) * OWN, (h // 2 + 1) * OWN)
        lanes = slice((h % 2) * HEAD, (h % 2 + 1) * HEAD)
        queries.append(rope(total[rows, lanes] * own_inverse, cosine[HALO:], sine[HALO:]))
    queries = jnp.concatenate(queries, axis=0)
    scores = lax.dot_general(queries, keys, (((1,), (1,)), ((), ())), preferred_element_type=f32)
    raised = jnp.where(mask_ref[...] > 0.0, jnp.exp(scores * (HEAD**-0.5)), 0.0)
    weights = (raised / jnp.sum(raised, axis=1, keepdims=True)).astype(bf16)
    mixed = jnp.dot(weights, values, preferred_element_type=f32).astype(bf16)
    for d in range(CHIPS):
        for h in range(4):
            out_ref[d, :, h * HEAD : (h + 1) * HEAD] = mixed[h * OWN : (h + 1) * OWN]


def out_kernel(mixed_ref, near_ref, far_ref, out_ref):
    mixed = mixed_ref[...]
    half = near_ref.shape[2]
    out_ref[:, :half] = jnp.dot(mixed, near_ref[0], preferred_element_type=f32).astype(bf16)
    out_ref[:, half:] = jnp.dot(mixed, far_ref[0], preferred_element_type=f32).astype(bf16)


def spread(mixed, near, far, layer):
    return pl.pallas_call(
        out_kernel,
        out_shape=jax.ShapeDtypeStruct((TOK, 1024), bf16),
        grid=(1,),
        in_specs=[VMEM] + [pl.BlockSpec((1, 512, 512), lambda i: (layer, 0, 0))] * 2,
        out_specs=VMEM,
        compiler_params=PARAMS,
        cost_estimate=pl.CostEstimate(flops=2 * 256 * 512 * 1024, bytes_accessed=2_000_000, transcendentals=0),
    )(mixed, near, far)


def sum_kernel(recv_ref, held_ref, out_ref, own_ref):
    total = held_ref[...].astype(f32)
    for d in range(GRID):
        total = total + recv_ref[d].astype(f32)
    own = total.astype(bf16)
    own_ref[...] = own
    for d in range(GRID):
        out_ref[d] = own


def weigh_kernel(query_ref, pair_ref, gain_ref, out_ref):
    rows = lax.broadcasted_iota(jnp.int32, (128, 128), 0)
    cols = lax.broadcasted_iota(jnp.int32, (128, 128), 1)
    scale = jnp.sum(jnp.where(rows == cols, gain_ref[...], 0.0), axis=1, keepdims=True)
    for d in range(4):
        query = query_ref[0, :, 512 * d : 512 * (d + 1)]
        pair = pair_ref[0, :, 256 * (d // 2) : 256 * (d // 2 + 1)]
        out_ref[d, :, :512] = (query.astype(f32) * scale).astype(bf16)
        out_ref[d, :, 512:] = (pair.astype(f32) * scale).astype(bf16)


def weigh(w_query, w_pair, gain):
    return pl.pallas_call(
        weigh_kernel,
        out_shape=jax.ShapeDtypeStruct((4, 512, 768), bf16),
        grid=(4,),
        in_specs=[
            pl.BlockSpec((1, 128, 2048), lambda i: (0, i, 0)),
            pl.BlockSpec((1, 128, 512), lambda i: (0, i, 0)),
            pl.BlockSpec((1, 128), lambda i: (0, i)),
        ],
        out_specs=pl.BlockSpec((4, 128, 768), lambda i: (0, i, 0)),
        compiler_params=STREAM,
        cost_estimate=pl.CostEstimate(flops=2_000_000, bytes_accessed=6_000_000, transcendentals=0),
    )(w_query, w_pair, gain)


def choose(arrays, is_index):
    chosen = arrays[0]
    for i in range(1, len(arrays)):
        chosen = jnp.where(is_index[i], arrays[i], chosen)
    return chosen


def rotated(value, steps):
    return lax.ppermute(value, "section", [(s, (s + steps) % 4) for s in range(4)])


def segment_info(lengths_row, total):
    token_ids = jnp.arange(total, dtype=jnp.int32)
    ends = jnp.cumsum(lengths_row)
    after = (token_ids[:, None] >= ends[None, :]).astype(jnp.int32)
    seg_ids = jnp.sum(after, axis=1)
    starts = jnp.sum(after * lengths_row[None, :], axis=1)
    return (seg_ids, token_ids - starts)


def swap(value):
    return lax.ppermute(value, "core", [(0, 1), (1, 0)])


def exchange(value, axis):
    return lax.all_to_all(value, axis, 0, 0, tiled=True)


def local(hidden_in, lengths, gain, w_query, w_pair, w_out):
    section = lax.axis_index("section")
    place = lax.axis_index("z")
    core = lax.axis_index("core")
    grid_place = section * 4 + lax.axis_index("row")

    near_in = exchange(weigh(w_query, w_pair, gain), "section")
    far_first = swap(near_in[:1])
    blocks_out = [lax.dynamic_slice(w_out, (0, 512 * ((section + k) % 4), 0), (1, 512, 512))[0] for k in range(4)]
    turn = [(section - layer) % 4 for layer in range(LAYERS)]

    mine = lax.dynamic_index_in_dim(hidden_in, core, 0, keepdims=False)
    theirs = lax.dynamic_index_in_dim(hidden_in, 1 - core, 0, keepdims=False)
    x = jnp.concatenate([mine, swap(theirs)], axis=1)
    held = lax.dynamic_slice_in_dim(x, grid_place * PART, PART, 0)

    seg, pos = segment_info(lax.dynamic_index_in_dim(lengths, core, 0, keepdims=False), TOK)
    seg_window = lax.dynamic_slice_in_dim(jnp.pad(seg, (HALO, 0), constant_values=-1), place * OWN, WINDOW)
    pos_window = lax.dynamic_slice_in_dim(jnp.pad(pos, (HALO, 0)), place * OWN, WINDOW)
    exponent = jnp.arange(HEAD // 2, dtype=f32) * (2.0 / HEAD)
    freqs = jnp.power(f32(ROPE_BASE), -exponent)
    angles = pos_window.astype(f32)[:, None] * freqs[None, :]
    cosine = jnp.cos(angles)
    sine = jnp.sin(angles)
    cosine = jnp.concatenate([cosine, cosine], axis=1)
    sine = jnp.concatenate([-sine, sine], axis=1)
    allowed = (seg_window[HALO:, None] == seg_window[None, :]) & (pos_window[None, :] <= pos_window[HALO:, None])
    mask = jnp.tile(allowed.astype(f32), (4, 1))
    place_arg = place.reshape(1).astype(jnp.int32)

    def attend(recv):
        return pl.pallas_call(
            attend_kernel,
            out_shape=jax.ShapeDtypeStruct((CHIPS, OWN, 512), bf16),
            in_specs=[pl.BlockSpec(memory_space=pltpu.SMEM)] + [VMEM] * 4,
            out_specs=VMEM,
            compiler_params=PARAMS,
            cost_estimate=pl.CostEstimate(flops=10_000_000, bytes_accessed=1_000_000, transcendentals=20_000),
        )(place_arg, recv, cosine, sine, mask)

    is_section = [(section == layer).astype(jnp.int32).reshape(1) for layer in range(LAYERS)]
    is_turn = [[turn[layer] == k for k in range(4)] for layer in range(LAYERS)]
    near_in, x, held, cosine, sine, mask, place_arg, is_section, is_turn, blocks_out = lax.optimization_barrier(
        (near_in, x, held, cosine, sine, mask, place_arg, is_section, is_turn, blocks_out)
    )
    moved_out = [blocks_out[0]] + [rotated(blocks_out[k], k) for k in range(1, 4)]
    kept = None
    for layer in range(LAYERS):
        if layer == 0:
            (packed,) = project(x, near_in, far_first, 0, 0, None, None)
        elif layer == 1:
            (packed,) = project(x, near_in, far_in, layer, layer, None, None)
            kept = x
        else:
            packed, kept = project(x, near_in, far_in, layer, layer, kept, is_section[layer - 1])
        copies = attend(exchange(packed, "z"))
        if layer == 0:
            copies, moved_out, rest = lax.optimization_barrier((copies, moved_out, near_in))
            near_out = jnp.stack([choose(moved_out, is_turn[each]) for each in range(LAYERS)])
            far_out = swap(near_out)
            far_in = swap(rest)
        mixed = exchange(copies, "z").reshape(TOK, 512)
        branch = spread(mixed, near_out, far_out, layer)
        copies, held = call(
            sum_kernel,
            (jax.ShapeDtypeStruct((GRID, PART, 1024), bf16), jax.ShapeDtypeStruct((PART, 1024), bf16)),
            (exchange(branch.reshape(GRID, PART, 1024), ("section", "row")), held),
            256 * 1024,
        )
        x = exchange(copies, ("section", "row")).reshape(TOK, 1024)

    kept = jnp.where(is_section[LAYERS - 1] == 1, x, kept)
    ours = kept[:, :512]
    other = swap(kept[:, 512:])
    final = jnp.where(core == 0, jnp.stack([ours, other]), jnp.stack([other, ours]))
    return final[None]


def solution(mesh):
    split = Mesh(mesh.devices.reshape(4, 4, 8, 2), ("section", "row", "z", "core"))
    col = ("z", "core")
    in_specs = (
        P(None, None, col),
        P(),
        P("section", col),
        P("section", col, "row"),
        P("section", col, "row"),
        P("section", "row", col),
    )
    out_specs = P("section", None, None, col)
    return jax.shard_map(local, mesh=split, in_specs=in_specs, out_specs=out_specs, check_vma=False)
```

```python
import jax
import jax.numpy as jnp
from jax import lax
from jax.experimental import pallas as pl
from jax.experimental.pallas import tpu as pltpu
from jax.sharding import Mesh
from jax.sharding import PartitionSpec as P

HEAD = 128
WIDTH = 8192
TOK = 256
LAYERS = 4
ROPE_BASE = 500000.0
EPSILON = 1e-05

CHIPS = 8
OWN = TOK // CHIPS
HALO = 64
WINDOW = HALO + OWN
PACK = 2 * OWN + WINDOW
GRID = 16
PART = TOK // GRID

bf16 = jnp.bfloat16
f32 = jnp.float32
VMEM = pl.BlockSpec(memory_space=pltpu.VMEM)
PARAMS = pltpu.CompilerParams(vmem_limit_bytes=12 * 1024 * 1024)
STREAM = pltpu.CompilerParams(vmem_limit_bytes=56 * 1024 * 1024)


def call(kernel, outs, args, flops):
    nbytes = sum(a.size * a.dtype.itemsize for a in args)
    return pl.pallas_call(
        kernel,
        out_shape=outs,
        in_specs=[VMEM] * len(args),
        out_specs=jax.tree.map(lambda _: VMEM, outs),
        compiler_params=PARAMS,
        cost_estimate=pl.CostEstimate(flops=flops, bytes_accessed=nbytes, transcendentals=0),
    )(*args)


def project(x, near, far, layer, far_layer, kept, flag):
    rows = 256
    outs = [jax.ShapeDtypeStruct((CHIPS, PACK, 256), bf16)]
    args = [x, near, far]
    in_specs = [
        VMEM,
        pl.BlockSpec((1, rows, 768), lambda i: (layer, i, 0)),
        pl.BlockSpec((1, rows, 768), lambda i: (far_layer, i, 0)),
    ]
    if kept is not None:
        outs.append(jax.ShapeDtypeStruct(kept.shape, bf16))
        args += [kept, flag]
        in_specs += [VMEM, pl.BlockSpec(memory_space=pltpu.SMEM)]
    return pl.pallas_call(
        project_kernel if kept is not None else first_project_kernel,
        out_shape=outs,
        grid=(2,),
        in_specs=in_specs,
        out_specs=[VMEM] * len(outs),
        scratch_shapes=[pltpu.VMEM((TOK, 768), f32)],
        compiler_params=PARAMS,
        cost_estimate=pl.CostEstimate(flops=2 * 256 * 1024 * 1024, bytes_accessed=3_000_000, transcendentals=0),
    )(*args)


def first_project_kernel(x_ref, near_ref, far_ref, out_ref, sum_ref):
    project_step(x_ref, near_ref, far_ref, out_ref, sum_ref)


def project_kernel(x_ref, near_ref, far_ref, kept_ref, flag_ref, out_ref, next_ref, sum_ref):
    project_step(x_ref, near_ref, far_ref, out_ref, sum_ref)

    @pl.when(pl.program_id(0) == 0)
    def _():
        next_ref[...] = jnp.where(flag_ref[0] == 1, x_ref[...], kept_ref[...])


def project_step(x_ref, near_ref, far_ref, out_ref, sum_ref):
    step = pl.program_id(0)
    near_x = x_ref[:, pl.ds(pl.multiple_of(step * 256, 256), 256)]
    far_x = x_ref[:, pl.ds(pl.multiple_of(512 + step * 256, 256), 256)]
    part = jnp.dot(near_x, near_ref[0], preferred_element_type=f32)
    part = part + jnp.dot(far_x, far_ref[0], preferred_element_type=f32)

    @pl.when(step == 0)
    def _():
        sum_ref[...] = part

    @pl.when(step == 1)
    def _():
        pack(x_ref[...], sum_ref[...] + part, out_ref)


def pack(x, y, out_ref):
    gram = lax.dot_general(x, x, (((1,), (1,)), ((), ())), preferred_element_type=f32)
    rows = lax.broadcasted_iota(jnp.int32, gram.shape, 0)
    cols = lax.broadcasted_iota(jnp.int32, gram.shape, 1)
    squares = jnp.sum(jnp.where(rows == cols, gram, 0.0), axis=0, keepdims=True)
    first = lax.broadcasted_iota(jnp.int32, (16, TOK), 0) == 0
    kv = y[:, 512:768]
    zero = jnp.zeros((16, TOK), f32)
    for d in range(CHIPS):
        own = slice(OWN * d, OWN * (d + 1))
        out_ref[d, 0:OWN, :] = y[own, 0:256].astype(bf16)
        out_ref[d, OWN : 2 * OWN, :] = y[own, 256:512].astype(bf16)
        begin = OWN * d - HALO
        for r in range(0, WINDOW, 16):
            t = begin + r
            block = kv[t : t + 16] if t >= 0 else zero
            if r == 0:
                block = jnp.where(first, squares, block)
            out_ref[d, 2 * OWN + r : 2 * OWN + r + 16, :] = block.astype(bf16)


def attend_kernel(place_ref, recv_ref, cos_ref, sin_ref, mask_ref, out_ref):
    total = recv_ref[0].astype(f32)
    for d in range(1, CHIPS):
        total = total + recv_ref[d].astype(f32)
    squares = total[2 * OWN : 2 * OWN + 1, :]
    inverse_row = lax.rsqrt(squares * (1.0 / WIDTH) + EPSILON)
    token = lax.broadcasted_iota(jnp.int32, (WINDOW, TOK), 0) + (place_ref[0] * OWN - HALO)
    lane = lax.broadcasted_iota(jnp.int32, (WINDOW, TOK), 1)
    inverse = jnp.sum(jnp.where(token == lane, inverse_row, 0.0), axis=1, keepdims=True)
    cosine = cos_ref[...]
    sine = sin_ref[...]

    def rope(v, c, s):
        return (v * c + pltpu.roll(v, HEAD // 2, 1) * s).astype(bf16)

    scaled = total[2 * OWN :, :] * inverse
    keys = rope(scaled[:, :HEAD], cosine, sine)
    values = scaled[:, HEAD:].astype(bf16)
    own_inverse = inverse[HALO:]
    queries = []
    for h in range(4):
        rows = slice((h // 2) * OWN, (h // 2 + 1) * OWN)
        lanes = slice((h % 2) * HEAD, (h % 2 + 1) * HEAD)
        queries.append(rope(total[rows, lanes] * own_inverse, cosine[HALO:], sine[HALO:]))
    queries = jnp.concatenate(queries, axis=0)
    scores = lax.dot_general(queries, keys, (((1,), (1,)), ((), ())), preferred_element_type=f32)
    raised = jnp.where(mask_ref[...] > 0.0, jnp.exp(scores * (HEAD**-0.5)), 0.0)
    weights = (raised / jnp.sum(raised, axis=1, keepdims=True)).astype(bf16)
    mixed = jnp.dot(weights, values, preferred_element_type=f32).astype(bf16)
    for d in range(CHIPS):
        for h in range(4):
            out_ref[d, :, h * HEAD : (h + 1) * HEAD] = mixed[h * OWN : (h + 1) * OWN]


def out_kernel(mixed_ref, near_ref, far_ref, out_ref):
    mixed = mixed_ref[...]
    half = near_ref.shape[2]
    out_ref[:, :half] = jnp.dot(mixed, near_ref[0], preferred_element_type=f32).astype(bf16)
    out_ref[:, half:] = jnp.dot(mixed, far_ref[0], preferred_element_type=f32).astype(bf16)


def spread(mixed, near, far, layer):
    return pl.pallas_call(
        out_kernel,
        out_shape=jax.ShapeDtypeStruct((TOK, 1024), bf16),
        grid=(1,),
        in_specs=[VMEM] + [pl.BlockSpec((1, 512, 512), lambda i: (layer, 0, 0))] * 2,
        out_specs=VMEM,
        compiler_params=PARAMS,
        cost_estimate=pl.CostEstimate(flops=2 * 256 * 512 * 1024, bytes_accessed=2_000_000, transcendentals=0),
    )(mixed, near, far)


def sum_kernel(recv_ref, held_ref, out_ref, own_ref):
    total = held_ref[...].astype(f32)
    for d in range(GRID):
        total = total + recv_ref[d].astype(f32)
    own = total.astype(bf16)
    own_ref[...] = own
    for d in range(GRID):
        out_ref[d] = own


def weigh_kernel(query_ref, pair_ref, gain_ref, out_ref):
    rows = lax.broadcasted_iota(jnp.int32, (128, 128), 0)
    cols = lax.broadcasted_iota(jnp.int32, (128, 128), 1)
    scale = jnp.sum(jnp.where(rows == cols, gain_ref[...], 0.0), axis=1, keepdims=True)
    for d in range(4):
        query = query_ref[0, :, 512 * d : 512 * (d + 1)]
        pair = pair_ref[0, :, 256 * (d // 2) : 256 * (d // 2 + 1)]
        out_ref[d, :, :512] = (query.astype(f32) * scale).astype(bf16)
        out_ref[d, :, 512:] = (pair.astype(f32) * scale).astype(bf16)


def weigh(w_query, w_pair, gain):
    return pl.pallas_call(
        weigh_kernel,
        out_shape=jax.ShapeDtypeStruct((4, 512, 768), bf16),
        grid=(4,),
        in_specs=[
            pl.BlockSpec((1, 128, 2048), lambda i: (0, i, 0)),
            pl.BlockSpec((1, 128, 512), lambda i: (0, i, 0)),
            pl.BlockSpec((1, 128), lambda i: (0, i)),
        ],
        out_specs=pl.BlockSpec((4, 128, 768), lambda i: (0, i, 0)),
        compiler_params=STREAM,
        cost_estimate=pl.CostEstimate(flops=2_000_000, bytes_accessed=6_000_000, transcendentals=0),
    )(w_query, w_pair, gain)


def choose(arrays, is_index):
    chosen = arrays[0]
    for i in range(1, len(arrays)):
        chosen = jnp.where(is_index[i], arrays[i], chosen)
    return chosen


def rotated(value, steps):
    return lax.ppermute(value, "section", [(s, (s + steps) % 4) for s in range(4)])


def segment_info(lengths_row, total):
    token_ids = jnp.arange(total, dtype=jnp.int32)
    ends = jnp.cumsum(lengths_row)
    after = (token_ids[:, None] >= ends[None, :]).astype(jnp.int32)
    seg_ids = jnp.sum(after, axis=1)
    starts = jnp.sum(after * lengths_row[None, :], axis=1)
    return (seg_ids, token_ids - starts)


def swap(value):
    return lax.ppermute(value, "core", [(0, 1), (1, 0)])


def exchange(value, axis):
    return lax.all_to_all(value, axis, 0, 0, tiled=True)


def local(hidden_in, lengths, gain, w_query, w_pair, w_out):
    section = lax.axis_index("section")
    place = lax.axis_index("z")
    core = lax.axis_index("core")
    grid_place = section * 4 + lax.axis_index("row")

    near_in = exchange(weigh(w_query, w_pair, gain), "section")
    blocks_out = [lax.dynamic_slice(w_out, (0, 512 * ((section + k) % 4), 0), (1, 512, 512))[0] for k in range(4)]
    turn = [(section - layer) % 4 for layer in range(LAYERS)]

    mine = lax.dynamic_index_in_dim(hidden_in, core, 0, keepdims=False)
    theirs = lax.dynamic_index_in_dim(hidden_in, 1 - core, 0, keepdims=False)
    x = jnp.concatenate([mine, swap(theirs)], axis=1)
    held = lax.dynamic_slice_in_dim(x, grid_place * PART, PART, 0)

    seg, pos = segment_info(lax.dynamic_index_in_dim(lengths, core, 0, keepdims=False), TOK)
    seg_window = lax.dynamic_slice_in_dim(jnp.pad(seg, (HALO, 0), constant_values=-1), place * OWN, WINDOW)
    pos_window = lax.dynamic_slice_in_dim(jnp.pad(pos, (HALO, 0)), place * OWN, WINDOW)
    exponent = jnp.arange(HEAD // 2, dtype=f32) * (2.0 / HEAD)
    freqs = jnp.power(f32(ROPE_BASE), -exponent)
    angles = pos_window.astype(f32)[:, None] * freqs[None, :]
    cosine = jnp.cos(angles)
    sine = jnp.sin(angles)
    cosine = jnp.concatenate([cosine, cosine], axis=1)
    sine = jnp.concatenate([-sine, sine], axis=1)
    allowed = (seg_window[HALO:, None] == seg_window[None, :]) & (pos_window[None, :] <= pos_window[HALO:, None])
    mask = jnp.tile(allowed.astype(f32), (4, 1))
    place_arg = place.reshape(1).astype(jnp.int32)

    def attend(recv):
        return pl.pallas_call(
            attend_kernel,
            out_shape=jax.ShapeDtypeStruct((CHIPS, OWN, 512), bf16),
            in_specs=[pl.BlockSpec(memory_space=pltpu.SMEM)] + [VMEM] * 4,
            out_specs=VMEM,
            compiler_params=PARAMS,
            cost_estimate=pl.CostEstimate(flops=10_000_000, bytes_accessed=1_000_000, transcendentals=20_000),
        )(place_arg, recv, cosine, sine, mask)

    is_section = [(section == layer).astype(jnp.int32).reshape(1) for layer in range(LAYERS)]
    is_turn = [[turn[layer] == k for k in range(4)] for layer in range(LAYERS)]
    near_in, x, held, cosine, sine, mask, place_arg, is_section, is_turn, blocks_out = lax.optimization_barrier(
        (near_in, x, held, cosine, sine, mask, place_arg, is_section, is_turn, blocks_out)
    )
    far_first = swap(near_in[:1])
    def mix(packed):
        return attend(exchange(packed, "z"))

    moved_out = [blocks_out[0]] + [rotated(blocks_out[k], k) for k in range(1, 4)]
    kept = None
    for layer in range(LAYERS):
        if layer == 0:
            (packed,) = project(x, near_in, far_first, 0, 0, None, None)
        elif layer == 1:
            (packed,) = project(x, near_in, far_in, layer, layer, None, None)
            kept = x
        else:
            packed, kept = project(x, near_in, far_in, layer, layer, kept, is_section[layer - 1])
        if layer == 0:
            copies = lax.cond(lengths[0, 0] > 0, mix, lambda value: jnp.zeros((CHIPS, OWN, 512), bf16), packed)
            copies, moved_out, rest = lax.optimization_barrier((copies, moved_out, near_in))
            near_out = jnp.stack([choose(moved_out, is_turn[each]) for each in range(LAYERS)])
            copies, near_out = lax.optimization_barrier((copies, near_out))
            far_out = swap(near_out)
            far_in = swap(rest)
        else:
            copies = mix(packed)
        mixed = exchange(copies, "z").reshape(TOK, 512)
        branch = spread(mixed, near_out, far_out, layer)
        copies, held = call(
            sum_kernel,
            (jax.ShapeDtypeStruct((GRID, PART, 1024), bf16), jax.ShapeDtypeStruct((PART, 1024), bf16)),
            (exchange(branch.reshape(GRID, PART, 1024), ("section", "row")), held),
            256 * 1024,
        )
        x = exchange(copies, ("section", "row")).reshape(TOK, 1024)

    kept = jnp.where(is_section[LAYERS - 1] == 1, x, kept)
    ours = kept[:, :512]
    other = swap(kept[:, 512:])
    final = jnp.where(core == 0, jnp.stack([ours, other]), jnp.stack([other, ours]))
    return final[None]


def solution(mesh):
    split = Mesh(mesh.devices.reshape(4, 4, 8, 2), ("section", "row", "z", "core"))
    col = ("z", "core")
    in_specs = (
        P(None, None, col),
        P(),
        P("section", col),
        P("section", col, "row"),
        P("section", col, "row"),
        P("section", "row", col),
    )
    out_specs = P("section", None, None, col)
    return jax.shard_map(local, mesh=split, in_specs=in_specs, out_specs=out_specs, check_vma=False)
```

```python
import jax
import jax.numpy as jnp
from jax import lax
from jax.experimental import pallas as pl
from jax.experimental.pallas import tpu as pltpu
from jax.sharding import Mesh
from jax.sharding import PartitionSpec as P

HEAD = 128
WIDTH = 8192
TOK = 256
LAYERS = 4
ROPE_BASE = 500000.0
EPSILON = 1e-05

CHIPS = 8
OWN = TOK // CHIPS
HALO = 64
WINDOW = HALO + OWN
PACK = 2 * OWN + WINDOW
GRID = 16
PART = TOK // GRID

bf16 = jnp.bfloat16
f32 = jnp.float32
VMEM = pl.BlockSpec(memory_space=pltpu.VMEM)
PARAMS = pltpu.CompilerParams(vmem_limit_bytes=12 * 1024 * 1024)
STREAM = pltpu.CompilerParams(vmem_limit_bytes=56 * 1024 * 1024)


def call(kernel, outs, args, flops):
    nbytes = sum(a.size * a.dtype.itemsize for a in args)
    return pl.pallas_call(
        kernel,
        out_shape=outs,
        in_specs=[VMEM] * len(args),
        out_specs=jax.tree.map(lambda _: VMEM, outs),
        compiler_params=PARAMS,
        cost_estimate=pl.CostEstimate(flops=flops, bytes_accessed=nbytes, transcendentals=0),
    )(*args)


def project(x, near, far, layer, far_layer, kept, flag):
    rows = 256
    outs = [jax.ShapeDtypeStruct((CHIPS, PACK, 256), bf16)]
    args = [x, near, far]
    in_specs = [
        VMEM,
        pl.BlockSpec((1, rows, 768), lambda i: (layer, i, 0)),
        pl.BlockSpec((1, rows, 768), lambda i: (far_layer, i, 0)),
    ]
    if kept is not None:
        outs.append(jax.ShapeDtypeStruct(kept.shape, bf16))
        args += [kept, flag]
        in_specs += [VMEM, pl.BlockSpec(memory_space=pltpu.SMEM)]
    return pl.pallas_call(
        project_kernel if kept is not None else first_project_kernel,
        out_shape=outs,
        grid=(2,),
        in_specs=in_specs,
        out_specs=[VMEM] * len(outs),
        scratch_shapes=[pltpu.VMEM((TOK, 768), f32)],
        compiler_params=PARAMS,
        cost_estimate=pl.CostEstimate(flops=2 * 256 * 1024 * 1024, bytes_accessed=3_000_000, transcendentals=0),
    )(*args)


def first_project_kernel(x_ref, near_ref, far_ref, out_ref, sum_ref):
    project_step(x_ref, near_ref, far_ref, out_ref, sum_ref)


def project_kernel(x_ref, near_ref, far_ref, kept_ref, flag_ref, out_ref, next_ref, sum_ref):
    project_step(x_ref, near_ref, far_ref, out_ref, sum_ref)

    @pl.when(pl.program_id(0) == 0)
    def _():
        next_ref[...] = jnp.where(flag_ref[0] == 1, x_ref[...], kept_ref[...])


def project_step(x_ref, near_ref, far_ref, out_ref, sum_ref):
    step = pl.program_id(0)
    near_x = x_ref[:, pl.ds(pl.multiple_of(step * 256, 256), 256)]
    far_x = x_ref[:, pl.ds(pl.multiple_of(512 + step * 256, 256), 256)]
    part = jnp.dot(near_x, near_ref[0], preferred_element_type=f32)
    part = part + jnp.dot(far_x, far_ref[0], preferred_element_type=f32)

    @pl.when(step == 0)
    def _():
        sum_ref[...] = part

    @pl.when(step == 1)
    def _():
        pack(x_ref[...], sum_ref[...] + part, out_ref)


def pack(x, y, out_ref):
    gram = lax.dot_general(x, x, (((1,), (1,)), ((), ())), preferred_element_type=f32)
    rows = lax.broadcasted_iota(jnp.int32, gram.shape, 0)
    cols = lax.broadcasted_iota(jnp.int32, gram.shape, 1)
    squares = jnp.sum(jnp.where(rows == cols, gram, 0.0), axis=0, keepdims=True)
    first = lax.broadcasted_iota(jnp.int32, (16, TOK), 0) == 0
    kv = y[:, 512:768]
    zero = jnp.zeros((16, TOK), f32)
    for d in range(CHIPS):
        own = slice(OWN * d, OWN * (d + 1))
        out_ref[d, 0:OWN, :] = y[own, 0:256].astype(bf16)
        out_ref[d, OWN : 2 * OWN, :] = y[own, 256:512].astype(bf16)
        begin = OWN * d - HALO
        for r in range(0, WINDOW, 16):
            t = begin + r
            block = kv[t : t + 16] if t >= 0 else zero
            if r == 0:
                block = jnp.where(first, squares, block)
            out_ref[d, 2 * OWN + r : 2 * OWN + r + 16, :] = block.astype(bf16)


def attend_kernel(place_ref, recv_ref, cos_ref, sin_ref, mask_ref, out_ref):
    total = recv_ref[0].astype(f32)
    for d in range(1, CHIPS):
        total = total + recv_ref[d].astype(f32)
    squares = total[2 * OWN : 2 * OWN + 1, :]
    inverse_row = lax.rsqrt(squares * (1.0 / WIDTH) + EPSILON)
    token = lax.broadcasted_iota(jnp.int32, (WINDOW, TOK), 0) + (place_ref[0] * OWN - HALO)
    lane = lax.broadcasted_iota(jnp.int32, (WINDOW, TOK), 1)
    inverse = jnp.sum(jnp.where(token == lane, inverse_row, 0.0), axis=1, keepdims=True)
    cosine = cos_ref[...]
    sine = sin_ref[...]

    def rope(v, c, s):
        return (v * c + pltpu.roll(v, HEAD // 2, 1) * s).astype(bf16)

    scaled = total[2 * OWN :, :] * inverse
    keys = rope(scaled[:, :HEAD], cosine, sine)
    values = scaled[:, HEAD:].astype(bf16)
    own_inverse = inverse[HALO:]
    queries = []
    for h in range(4):
        rows = slice((h // 2) * OWN, (h // 2 + 1) * OWN)
        lanes = slice((h % 2) * HEAD, (h % 2 + 1) * HEAD)
        queries.append(rope(total[rows, lanes] * own_inverse, cosine[HALO:], sine[HALO:]))
    queries = jnp.concatenate(queries, axis=0)
    scores = lax.dot_general(queries, keys, (((1,), (1,)), ((), ())), preferred_element_type=f32)
    mask = jnp.concatenate([mask_ref[...]] * 4, axis=0)
    raised = jnp.where(mask > 0.0, jnp.exp(scores * (HEAD**-0.5)), 0.0)
    weights = (raised / jnp.sum(raised, axis=1, keepdims=True)).astype(bf16)
    mixed = jnp.dot(weights, values, preferred_element_type=f32).astype(bf16)
    for d in range(CHIPS):
        for h in range(4):
            out_ref[d, :, h * HEAD : (h + 1) * HEAD] = mixed[h * OWN : (h + 1) * OWN]


def out_kernel(mixed_ref, near_ref, far_ref, out_ref):
    mixed = mixed_ref[...]
    half = near_ref.shape[2]
    out_ref[:, :half] = jnp.dot(mixed, near_ref[0], preferred_element_type=f32).astype(bf16)
    out_ref[:, half:] = jnp.dot(mixed, far_ref[0], preferred_element_type=f32).astype(bf16)


def spread(mixed, near, far, layer):
    return pl.pallas_call(
        out_kernel,
        out_shape=jax.ShapeDtypeStruct((TOK, 1024), bf16),
        grid=(1,),
        in_specs=[VMEM] + [pl.BlockSpec((1, 512, 512), lambda i: (layer, 0, 0))] * 2,
        out_specs=VMEM,
        compiler_params=PARAMS,
        cost_estimate=pl.CostEstimate(flops=2 * 256 * 512 * 1024, bytes_accessed=2_000_000, transcendentals=0),
    )(mixed, near, far)


def sum_kernel(recv_ref, held_ref, out_ref, own_ref):
    total = held_ref[...].astype(f32)
    for d in range(GRID):
        total = total + recv_ref[d].astype(f32)
    own = total.astype(bf16)
    own_ref[...] = own
    for d in range(GRID):
        out_ref[d] = own


def weigh_kernel(query_ref, pair_ref, gain_ref, out_ref):
    rows = lax.broadcasted_iota(jnp.int32, (256, 256), 0)
    cols = lax.broadcasted_iota(jnp.int32, (256, 256), 1)
    scale = jnp.sum(jnp.where(rows == cols, gain_ref[...], 0.0), axis=1, keepdims=True)
    pair = (pair_ref[0].astype(f32) * scale).astype(bf16)
    for d in range(4):
        query = query_ref[0, :, 512 * d : 512 * (d + 1)]
        out_ref[d, :, :512] = (query.astype(f32) * scale).astype(bf16)
        out_ref[d, :, 512:] = pair[:, 256 * (d // 2) : 256 * (d // 2 + 1)]


def weigh(w_query, w_pair, gain):
    return pl.pallas_call(
        weigh_kernel,
        out_shape=jax.ShapeDtypeStruct((4, 512, 768), bf16),
        grid=(2,),
        in_specs=[
            pl.BlockSpec((1, 256, 2048), lambda i: (0, i, 0)),
            pl.BlockSpec((1, 256, 512), lambda i: (0, i, 0)),
            pl.BlockSpec((1, 256), lambda i: (0, i)),
        ],
        out_specs=pl.BlockSpec((4, 256, 768), lambda i: (0, i, 0)),
        compiler_params=STREAM,
        cost_estimate=pl.CostEstimate(flops=2_000_000, bytes_accessed=6_000_000, transcendentals=0),
    )(w_query, w_pair, gain)


def choose(arrays, is_index):
    chosen = arrays[0]
    for i in range(1, len(arrays)):
        chosen = jnp.where(is_index[i], arrays[i], chosen)
    return chosen


def rotated(value, steps):
    return lax.ppermute(value, "section", [(s, (s + steps) % 4) for s in range(4)])


def segment_info(lengths_row, total):
    token_ids = jnp.arange(total, dtype=jnp.int32)
    ends = jnp.cumsum(lengths_row)
    after = (token_ids[:, None] >= ends[None, :]).astype(jnp.int32)
    seg_ids = jnp.sum(after, axis=1)
    starts = jnp.sum(after * lengths_row[None, :], axis=1)
    return (seg_ids, token_ids - starts)


def swap(value):
    return lax.ppermute(value, "core", [(0, 1), (1, 0)])


def exchange(value, axis):
    return lax.all_to_all(value, axis, 0, 0, tiled=True)


def local(hidden_in, lengths, gain, w_query, w_pair, w_out):
    section = lax.axis_index("section")
    place = lax.axis_index("z")
    core = lax.axis_index("core")
    grid_place = section * 4 + lax.axis_index("row")

    near_in = exchange(weigh(w_query, w_pair, gain), "section")
    blocks_out = [lax.dynamic_slice(w_out, (0, 512 * ((section + k) % 4), 0), (1, 512, 512))[0] for k in range(4)]
    turn = [(section - layer) % 4 for layer in range(LAYERS)]

    mine = lax.dynamic_index_in_dim(hidden_in, core, 0, keepdims=False)
    theirs = lax.dynamic_index_in_dim(hidden_in, 1 - core, 0, keepdims=False)
    x = jnp.concatenate([mine, swap(theirs)], axis=1)
    held = lax.dynamic_slice_in_dim(x, grid_place * PART, PART, 0)

    seg, pos = segment_info(lax.dynamic_index_in_dim(lengths, core, 0, keepdims=False), TOK)
    seg_window = lax.dynamic_slice_in_dim(jnp.pad(seg, (HALO, 0), constant_values=-1), place * OWN, WINDOW)
    pos_window = lax.dynamic_slice_in_dim(jnp.pad(pos, (HALO, 0)), place * OWN, WINDOW)
    exponent = jnp.arange(HEAD // 2, dtype=f32) * (2.0 / HEAD)
    freqs = jnp.power(f32(ROPE_BASE), -exponent)
    angles = pos_window.astype(f32)[:, None] * freqs[None, :]
    cosine = jnp.cos(angles)
    sine = jnp.sin(angles)
    cosine = jnp.concatenate([cosine, cosine], axis=1)
    sine = jnp.concatenate([-sine, sine], axis=1)
    allowed = (seg_window[HALO:, None] == seg_window[None, :]) & (pos_window[None, :] <= pos_window[HALO:, None])
    mask = allowed.astype(f32)
    place_arg = place.reshape(1).astype(jnp.int32)

    def attend(recv):
        return pl.pallas_call(
            attend_kernel,
            out_shape=jax.ShapeDtypeStruct((CHIPS, OWN, 512), bf16),
            in_specs=[pl.BlockSpec(memory_space=pltpu.SMEM)] + [VMEM] * 4,
            out_specs=VMEM,
            compiler_params=PARAMS,
            cost_estimate=pl.CostEstimate(flops=10_000_000, bytes_accessed=1_000_000, transcendentals=20_000),
        )(place_arg, recv, cosine, sine, mask)

    is_section = [(section == layer).astype(jnp.int32).reshape(1) for layer in range(LAYERS)]
    is_turn = [[turn[layer] == k for k in range(4)] for layer in range(LAYERS)]
    is_first = lengths[0, 0] > 0
    is_last = section == LAYERS - 1
    is_core = core == 0
    near_in, x, held, cosine, sine, mask, place_arg, is_first, is_last, is_core, is_section, is_turn, blocks_out = (
        lax.optimization_barrier(
            (near_in, x, held, cosine, sine, mask, place_arg, is_first, is_last, is_core, is_section, is_turn, blocks_out)
        )
    )
    def mix(packed):
        return attend(exchange(packed, "z"))

    def begin(x, near_in, far_first):
        (packed,) = project(x, near_in, far_first, 0, 0, None, None)
        return mix(packed)

    far_first = swap(near_in[:1])
    moved_out = [blocks_out[0]] + [rotated(blocks_out[k], k) for k in range(1, 4)]
    kept = None
    for layer in range(LAYERS):
        if layer == 1:
            (packed,) = project(x, near_in, far_in, layer, layer, None, None)
            kept = x
        elif layer > 1:
            packed, kept = project(x, near_in, far_in, layer, layer, kept, is_section[layer - 1])
        if layer == 0:
            copies = lax.cond(is_first, begin, lambda *_: jnp.zeros((CHIPS, OWN, 512), bf16), x, near_in, far_first)
            copies, moved_out, rest = lax.optimization_barrier((copies, moved_out, near_in))
            near_out = jnp.stack([choose(moved_out, is_turn[each]) for each in range(LAYERS)])
            copies, near_out = lax.optimization_barrier((copies, near_out))
            far_out = swap(near_out)
            far_in = swap(rest)
        else:
            copies = mix(packed)
        mixed = exchange(copies, "z").reshape(TOK, 512)
        branch = spread(mixed, near_out, far_out, layer)
        copies, held = call(
            sum_kernel,
            (jax.ShapeDtypeStruct((GRID, PART, 1024), bf16), jax.ShapeDtypeStruct((PART, 1024), bf16)),
            (exchange(branch.reshape(GRID, PART, 1024), ("section", "row")), held),
            256 * 1024,
        )
        x = exchange(copies, ("section", "row")).reshape(TOK, 1024)

    kept = jnp.where(is_last, x, kept)
    ours = kept[:, :512]
    other = swap(kept[:, 512:])
    final = jnp.where(is_core, jnp.stack([ours, other]), jnp.stack([other, ours]))
    return final[None]


def solution(mesh):
    split = Mesh(mesh.devices.reshape(4, 4, 8, 2), ("section", "row", "z", "core"))
    col = ("z", "core")
    in_specs = (
        P(None, None, col),
        P(),
        P("section", col),
        P("section", col, "row"),
        P("section", col, "row"),
        P("section", "row", col),
    )
    out_specs = P("section", None, None, col)
    return jax.shard_map(local, mesh=split, in_specs=in_specs, out_specs=out_specs, check_vma=False)
```

```python
import jax
import jax.numpy as jnp
from jax import lax
from jax.experimental import pallas as pl
from jax.experimental.pallas import tpu as pltpu
from jax.sharding import Mesh
from jax.sharding import PartitionSpec as P

HEAD = 128
WIDTH = 8192
TOK = 256
LAYERS = 4
ROPE_BASE = 500000.0
EPSILON = 1e-05

CHIPS = 8
OWN = TOK // CHIPS
HALO = 64
WINDOW = HALO + OWN
PACK = 2 * OWN + WINDOW
GRID = 16
PART = TOK // GRID

bf16 = jnp.bfloat16
f32 = jnp.float32
VMEM = pl.BlockSpec(memory_space=pltpu.VMEM)
PARAMS = pltpu.CompilerParams(vmem_limit_bytes=12 * 1024 * 1024)
PROJECT = pltpu.CompilerParams(vmem_limit_bytes=24 * 1024 * 1024)
STREAM = pltpu.CompilerParams(vmem_limit_bytes=56 * 1024 * 1024)


def call(kernel, outs, args, flops):
    nbytes = sum(a.size * a.dtype.itemsize for a in args)
    return pl.pallas_call(
        kernel,
        out_shape=outs,
        in_specs=[VMEM] * len(args),
        out_specs=jax.tree.map(lambda _: VMEM, outs),
        compiler_params=PARAMS,
        cost_estimate=pl.CostEstimate(flops=flops, bytes_accessed=nbytes, transcendentals=0),
    )(*args)


def project(x, near, far, layer, far_layer, kept, flag):
    outs = [jax.ShapeDtypeStruct((CHIPS, PACK, 256), bf16)]
    args = [x, near, far]
    in_specs = [VMEM] * 3
    if kept is not None:
        outs.append(jax.ShapeDtypeStruct(kept.shape, bf16))
        args += [kept, flag]
        in_specs += [VMEM, pl.BlockSpec(memory_space=pltpu.SMEM)]

    def kernel(x_ref, near_ref, far_ref, *refs):
        x = x_ref[...]
        half = x.shape[1] // 2
        y = jnp.dot(x[:, :half], near_ref[layer], preferred_element_type=f32)
        y = y + jnp.dot(x[:, half:], far_ref[far_layer], preferred_element_type=f32)
        if kept is None:
            (out_ref,) = refs
        else:
            kept_ref, flag_ref, out_ref, next_ref = refs
            next_ref[...] = jnp.where(flag_ref[0] == 1, x, kept_ref[...])
        pack(x, y, out_ref)

    return pl.pallas_call(
        kernel,
        out_shape=outs,
        in_specs=in_specs,
        out_specs=[VMEM] * len(outs),
        compiler_params=PROJECT,
        cost_estimate=pl.CostEstimate(flops=2 * 256 * 1024 * 1024, bytes_accessed=3_000_000, transcendentals=0),
    )(*args)


def pack(x, y, out_ref):
    gram = lax.dot_general(x, x, (((1,), (1,)), ((), ())), preferred_element_type=f32)
    rows = lax.broadcasted_iota(jnp.int32, gram.shape, 0)
    cols = lax.broadcasted_iota(jnp.int32, gram.shape, 1)
    squares = jnp.sum(jnp.where(rows == cols, gram, 0.0), axis=0, keepdims=True)
    first = lax.broadcasted_iota(jnp.int32, (16, TOK), 0) == 0
    kv = y[:, 512:768]
    zero = jnp.zeros((16, TOK), f32)
    for d in range(CHIPS):
        own = slice(OWN * d, OWN * (d + 1))
        out_ref[d, 0:OWN, :] = y[own, 0:256].astype(bf16)
        out_ref[d, OWN : 2 * OWN, :] = y[own, 256:512].astype(bf16)
        begin = OWN * d - HALO
        for r in range(0, WINDOW, 16):
            t = begin + r
            block = kv[t : t + 16] if t >= 0 else zero
            if r == 0:
                block = jnp.where(first, squares, block)
            out_ref[d, 2 * OWN + r : 2 * OWN + r + 16, :] = block.astype(bf16)


def attend_kernel(place_ref, recv_ref, cos_ref, sin_ref, mask_ref, out_ref):
    total = recv_ref[0].astype(f32)
    for d in range(1, CHIPS):
        total = total + recv_ref[d].astype(f32)
    squares = total[2 * OWN : 2 * OWN + 1, :]
    inverse_row = lax.rsqrt(squares * (1.0 / WIDTH) + EPSILON)
    token = lax.broadcasted_iota(jnp.int32, (WINDOW, TOK), 0) + (place_ref[0] * OWN - HALO)
    lane = lax.broadcasted_iota(jnp.int32, (WINDOW, TOK), 1)
    inverse = jnp.sum(jnp.where(token == lane, inverse_row, 0.0), axis=1, keepdims=True)
    cosine = cos_ref[...]
    sine = sin_ref[...]

    def rope(v, c, s):
        return (v * c + pltpu.roll(v, HEAD // 2, 1) * s).astype(bf16)

    scaled = total[2 * OWN :, :] * inverse
    keys = rope(scaled[:, :HEAD], cosine, sine)
    values = scaled[:, HEAD:].astype(bf16)
    own_inverse = inverse[HALO:]
    queries = []
    for h in range(4):
        rows = slice((h // 2) * OWN, (h // 2 + 1) * OWN)
        lanes = slice((h % 2) * HEAD, (h % 2 + 1) * HEAD)
        queries.append(rope(total[rows, lanes] * own_inverse, cosine[HALO:], sine[HALO:]))
    queries = jnp.concatenate(queries, axis=0)
    scores = lax.dot_general(queries, keys, (((1,), (1,)), ((), ())), preferred_element_type=f32)
    mask = jnp.concatenate([mask_ref[...]] * 4, axis=0)
    raised = jnp.where(mask > 0.0, jnp.exp(scores * (HEAD**-0.5)), 0.0)
    weights = (raised / jnp.sum(raised, axis=1, keepdims=True)).astype(bf16)
    mixed = jnp.dot(weights, values, preferred_element_type=f32).astype(bf16)
    for d in range(CHIPS):
        for h in range(4):
            out_ref[d, :, h * HEAD : (h + 1) * HEAD] = mixed[h * OWN : (h + 1) * OWN]


def out_kernel(mixed_ref, near_ref, far_ref, out_ref):
    mixed = mixed_ref[...]
    half = near_ref.shape[2]
    out_ref[:, :half] = jnp.dot(mixed, near_ref[0], preferred_element_type=f32).astype(bf16)
    out_ref[:, half:] = jnp.dot(mixed, far_ref[0], preferred_element_type=f32).astype(bf16)


def spread(mixed, near, far, layer):
    return pl.pallas_call(
        out_kernel,
        out_shape=jax.ShapeDtypeStruct((TOK, 1024), bf16),
        grid=(1,),
        in_specs=[VMEM] + [pl.BlockSpec((1, 512, 512), lambda i: (layer, 0, 0))] * 2,
        out_specs=VMEM,
        compiler_params=PARAMS,
        cost_estimate=pl.CostEstimate(flops=2 * 256 * 512 * 1024, bytes_accessed=2_000_000, transcendentals=0),
    )(mixed, near, far)


def sum_kernel(recv_ref, held_ref, out_ref, own_ref):
    total = held_ref[...].astype(f32)
    for d in range(GRID):
        total = total + recv_ref[d].astype(f32)
    own = total.astype(bf16)
    own_ref[...] = own
    for d in range(GRID):
        out_ref[d] = own


def weigh_kernel(query_ref, pair_ref, gain_ref, out_ref):
    rows = lax.broadcasted_iota(jnp.int32, (256, 256), 0)
    cols = lax.broadcasted_iota(jnp.int32, (256, 256), 1)
    scale = jnp.sum(jnp.where(rows == cols, gain_ref[...], 0.0), axis=1, keepdims=True)
    pair = (pair_ref[0].astype(f32) * scale).astype(bf16)
    for d in range(4):
        query = query_ref[0, :, 512 * d : 512 * (d + 1)]
        out_ref[d, :, :512] = (query.astype(f32) * scale).astype(bf16)
        out_ref[d, :, 512:] = pair[:, 256 * (d // 2) : 256 * (d // 2 + 1)]


def weigh(w_query, w_pair, gain):
    return pl.pallas_call(
        weigh_kernel,
        out_shape=jax.ShapeDtypeStruct((4, 512, 768), bf16),
        grid=(2,),
        in_specs=[
            pl.BlockSpec((1, 256, 2048), lambda i: (0, i, 0)),
            pl.BlockSpec((1, 256, 512), lambda i: (0, i, 0)),
            pl.BlockSpec((1, 256), lambda i: (0, i)),
        ],
        out_specs=pl.BlockSpec((4, 256, 768), lambda i: (0, i, 0)),
        compiler_params=STREAM,
        cost_estimate=pl.CostEstimate(flops=2_000_000, bytes_accessed=6_000_000, transcendentals=0),
    )(w_query, w_pair, gain)


def choose(arrays, is_index):
    chosen = arrays[0]
    for i in range(1, len(arrays)):
        chosen = jnp.where(is_index[i], arrays[i], chosen)
    return chosen


def rotated(value, steps):
    return lax.ppermute(value, "section", [(s, (s + steps) % 4) for s in range(4)])


def segment_info(lengths_row, total):
    token_ids = jnp.arange(total, dtype=jnp.int32)
    ends = jnp.cumsum(lengths_row)
    after = (token_ids[:, None] >= ends[None, :]).astype(jnp.int32)
    seg_ids = jnp.sum(after, axis=1)
    starts = jnp.sum(after * lengths_row[None, :], axis=1)
    return (seg_ids, token_ids - starts)


def swap(value):
    return lax.ppermute(value, "core", [(0, 1), (1, 0)])


def exchange(value, axis):
    return lax.all_to_all(value, axis, 0, 0, tiled=True)


def local(hidden_in, lengths, gain, w_query, w_pair, w_out):
    section = lax.axis_index("section")
    place = lax.axis_index("z")
    core = lax.axis_index("core")
    grid_place = section * 4 + lax.axis_index("row")

    near_in = exchange(weigh(w_query, w_pair, gain), "section")
    blocks_out = [lax.dynamic_slice(w_out, (0, 512 * ((section + k) % 4), 0), (1, 512, 512))[0] for k in range(4)]
    turn = [(section - layer) % 4 for layer in range(LAYERS)]

    mine = lax.dynamic_index_in_dim(hidden_in, core, 0, keepdims=False)
    theirs = lax.dynamic_index_in_dim(hidden_in, 1 - core, 0, keepdims=False)
    x = jnp.concatenate([mine, swap(theirs)], axis=1)
    held = lax.dynamic_slice_in_dim(x, grid_place * PART, PART, 0)

    seg, pos = segment_info(lax.dynamic_index_in_dim(lengths, core, 0, keepdims=False), TOK)
    seg_window = lax.dynamic_slice_in_dim(jnp.pad(seg, (HALO, 0), constant_values=-1), place * OWN, WINDOW)
    pos_window = lax.dynamic_slice_in_dim(jnp.pad(pos, (HALO, 0)), place * OWN, WINDOW)
    exponent = jnp.arange(HEAD // 2, dtype=f32) * (2.0 / HEAD)
    freqs = jnp.power(f32(ROPE_BASE), -exponent)
    angles = pos_window.astype(f32)[:, None] * freqs[None, :]
    cosine = jnp.cos(angles)
    sine = jnp.sin(angles)
    cosine = jnp.concatenate([cosine, cosine], axis=1)
    sine = jnp.concatenate([-sine, sine], axis=1)
    allowed = (seg_window[HALO:, None] == seg_window[None, :]) & (pos_window[None, :] <= pos_window[HALO:, None])
    mask = allowed.astype(f32)
    place_arg = place.reshape(1).astype(jnp.int32)

    def attend(recv):
        return pl.pallas_call(
            attend_kernel,
            out_shape=jax.ShapeDtypeStruct((CHIPS, OWN, 512), bf16),
            in_specs=[pl.BlockSpec(memory_space=pltpu.SMEM)] + [VMEM] * 4,
            out_specs=VMEM,
            compiler_params=PARAMS,
            cost_estimate=pl.CostEstimate(flops=10_000_000, bytes_accessed=1_000_000, transcendentals=20_000),
        )(place_arg, recv, cosine, sine, mask)

    is_section = [(section == layer).astype(jnp.int32).reshape(1) for layer in range(LAYERS)]
    is_turn = [[turn[layer] == k for k in range(4)] for layer in range(LAYERS)]
    is_first = lengths[0, 0] > 0
    is_last = section == LAYERS - 1
    is_core = core == 0
    near_in, x, held, cosine, sine, mask, place_arg, is_first, is_last, is_core, is_section, is_turn, blocks_out = (
        lax.optimization_barrier(
            (near_in, x, held, cosine, sine, mask, place_arg, is_first, is_last, is_core, is_section, is_turn, blocks_out)
        )
    )
    def mix(packed):
        return attend(exchange(packed, "z"))

    def begin(x, near_in, far_first):
        (packed,) = project(x, near_in, far_first, 0, 0, None, None)
        return mix(packed)

    far_first = swap(near_in[:1])
    moved_out = [blocks_out[0]] + [rotated(blocks_out[k], k) for k in range(1, 4)]
    kept = None
    for layer in range(LAYERS):
        if layer == 1:
            (packed,) = project(x, near_in, far_in, layer, layer, None, None)
            kept = x
        elif layer > 1:
            packed, kept = project(x, near_in, far_in, layer, layer, kept, is_section[layer - 1])
        if layer == 0:
            copies = lax.cond(is_first, begin, lambda *_: jnp.zeros((CHIPS, OWN, 512), bf16), x, near_in, far_first)
            copies, moved_out, rest = lax.optimization_barrier((copies, moved_out, near_in))
            near_out = jnp.stack([choose(moved_out, is_turn[each]) for each in range(LAYERS)])
            copies, near_out = lax.optimization_barrier((copies, near_out))
            far_out = swap(near_out)
            far_in = swap(rest)
        else:
            copies = mix(packed)
        mixed = exchange(copies, "z").reshape(TOK, 512)
        branch = spread(mixed, near_out, far_out, layer)
        copies, held = call(
            sum_kernel,
            (jax.ShapeDtypeStruct((GRID, PART, 1024), bf16), jax.ShapeDtypeStruct((PART, 1024), bf16)),
            (exchange(branch.reshape(GRID, PART, 1024), ("section", "row")), held),
            256 * 1024,
        )
        x = exchange(copies, ("section", "row")).reshape(TOK, 1024)

    kept = jnp.where(is_last, x, kept)
    ours = kept[:, :512]
    other = swap(kept[:, 512:])
    final = jnp.where(is_core, jnp.stack([ours, other]), jnp.stack([other, ours]))
    return final[None]


def solution(mesh):
    split = Mesh(mesh.devices.reshape(4, 4, 8, 2), ("section", "row", "z", "core"))
    col = ("z", "core")
    in_specs = (
        P(None, None, col),
        P(),
        P("section", col),
        P("section", col, "row"),
        P("section", col, "row"),
        P("section", "row", col),
    )
    out_specs = P("section", None, None, col)
    return jax.shard_map(local, mesh=split, in_specs=in_specs, out_specs=out_specs, check_vma=False)
```

```python
import jax
import jax.numpy as jnp
from jax import lax
from jax.experimental import pallas as pl
from jax.experimental.pallas import tpu as pltpu
from jax.sharding import Mesh
from jax.sharding import PartitionSpec as P

HEAD = 128
WIDTH = 8192
TOK = 256
LAYERS = 4
ROPE_BASE = 500000.0
EPSILON = 1e-05

CHIPS = 8
OWN = TOK // CHIPS
HALO = 64
WINDOW = HALO + OWN
PACK = 2 * OWN + WINDOW
GRID = 16
PART = TOK // GRID

bf16 = jnp.bfloat16
f32 = jnp.float32
VMEM = pl.BlockSpec(memory_space=pltpu.VMEM)
PARAMS = pltpu.CompilerParams(vmem_limit_bytes=12 * 1024 * 1024)
PROJECT = pltpu.CompilerParams(vmem_limit_bytes=24 * 1024 * 1024)
STREAM = pltpu.CompilerParams(vmem_limit_bytes=56 * 1024 * 1024)


def call(kernel, outs, args, flops):
    nbytes = sum(a.size * a.dtype.itemsize for a in args)
    return pl.pallas_call(
        kernel,
        out_shape=outs,
        in_specs=[VMEM] * len(args),
        out_specs=jax.tree.map(lambda _: VMEM, outs),
        compiler_params=PARAMS,
        cost_estimate=pl.CostEstimate(flops=flops, bytes_accessed=nbytes, transcendentals=0),
    )(*args)


def project(x, near, far, layer, far_layer, kept, flag):
    outs = [jax.ShapeDtypeStruct((CHIPS, PACK, 256), bf16)]
    args = [x, near, far]
    in_specs = [VMEM] * 3
    if kept is not None:
        outs.append(jax.ShapeDtypeStruct(kept.shape, bf16))
        args += [kept, flag]
        in_specs += [VMEM, pl.BlockSpec(memory_space=pltpu.SMEM)]

    def kernel(x_ref, near_ref, far_ref, *refs):
        x = x_ref[...]
        half = x.shape[1] // 2
        y = jnp.dot(x[:, :half], near_ref[layer], preferred_element_type=f32)
        y = y + jnp.dot(x[:, half:], far_ref[far_layer], preferred_element_type=f32)
        if kept is None:
            (out_ref,) = refs
        else:
            kept_ref, flag_ref, out_ref, next_ref = refs
            next_ref[...] = jnp.where(flag_ref[0] == 1, x, kept_ref[...])
        pack(x, y, out_ref)

    return pl.pallas_call(
        kernel,
        out_shape=outs,
        in_specs=in_specs,
        out_specs=[VMEM] * len(outs),
        compiler_params=PROJECT,
        cost_estimate=pl.CostEstimate(flops=2 * 256 * 1024 * 1024, bytes_accessed=3_000_000, transcendentals=0),
    )(*args)


def pack(x, y, out_ref):
    gram = lax.dot_general(x, x, (((1,), (1,)), ((), ())), preferred_element_type=f32)
    rows = lax.broadcasted_iota(jnp.int32, gram.shape, 0)
    cols = lax.broadcasted_iota(jnp.int32, gram.shape, 1)
    squares = jnp.sum(jnp.where(rows == cols, gram, 0.0), axis=0, keepdims=True)
    first = lax.broadcasted_iota(jnp.int32, (16, TOK), 0) == 0
    kv = y[:, 512:768]
    zero = jnp.zeros((16, TOK), f32)
    for d in range(CHIPS):
        own = slice(OWN * d, OWN * (d + 1))
        out_ref[d, 0:OWN, :] = y[own, 0:256].astype(bf16)
        out_ref[d, OWN : 2 * OWN, :] = y[own, 256:512].astype(bf16)
        begin = OWN * d - HALO
        for r in range(0, WINDOW, 16):
            t = begin + r
            block = kv[t : t + 16] if t >= 0 else zero
            if r == 0:
                block = jnp.where(first, squares, block)
            out_ref[d, 2 * OWN + r : 2 * OWN + r + 16, :] = block.astype(bf16)


def attend_kernel(place_ref, recv_ref, cos_ref, sin_ref, mask_ref, out_ref):
    total = recv_ref[0].astype(f32)
    for d in range(1, CHIPS):
        total = total + recv_ref[d].astype(f32)
    squares = total[2 * OWN : 2 * OWN + 1, :]
    inverse_row = lax.rsqrt(squares * (1.0 / WIDTH) + EPSILON)
    token = lax.broadcasted_iota(jnp.int32, (WINDOW, TOK), 0) + (place_ref[0] * OWN - HALO)
    lane = lax.broadcasted_iota(jnp.int32, (WINDOW, TOK), 1)
    inverse = jnp.sum(jnp.where(token == lane, inverse_row, 0.0), axis=1, keepdims=True)
    cosine = cos_ref[...]
    sine = sin_ref[...]

    def rope(v, c, s):
        return (v * c + pltpu.roll(v, HEAD // 2, 1) * s).astype(bf16)

    scaled = total[2 * OWN :, :] * inverse
    keys = rope(scaled[:, :HEAD], cosine, sine)
    values = scaled[:, HEAD:].astype(bf16)
    own_inverse = inverse[HALO:]
    queries = []
    for h in range(4):
        rows = slice((h // 2) * OWN, (h // 2 + 1) * OWN)
        lanes = slice((h % 2) * HEAD, (h % 2 + 1) * HEAD)
        queries.append(rope(total[rows, lanes] * own_inverse, cosine[HALO:], sine[HALO:]))
    queries = jnp.concatenate(queries, axis=0)
    scores = lax.dot_general(queries, keys, (((1,), (1,)), ((), ())), preferred_element_type=f32)
    mask = jnp.concatenate([mask_ref[...]] * 4, axis=0)
    raised = jnp.where(mask > 0.0, jnp.exp(scores * (HEAD**-0.5)), 0.0)
    weights = (raised / jnp.sum(raised, axis=1, keepdims=True)).astype(bf16)
    mixed = jnp.dot(weights, values, preferred_element_type=f32).astype(bf16)
    for d in range(CHIPS):
        for h in range(4):
            out_ref[d, :, h * HEAD : (h + 1) * HEAD] = mixed[h * OWN : (h + 1) * OWN]


def out_kernel(mixed_ref, near_ref, far_ref, out_ref):
    mixed = mixed_ref[...]
    half = near_ref.shape[2]
    out_ref[:, :half] = jnp.dot(mixed, near_ref[0], preferred_element_type=f32).astype(bf16)
    out_ref[:, half:] = jnp.dot(mixed, far_ref[0], preferred_element_type=f32).astype(bf16)


def spread(mixed, near, far, layer):
    return pl.pallas_call(
        out_kernel,
        out_shape=jax.ShapeDtypeStruct((TOK, 1024), bf16),
        grid=(1,),
        in_specs=[VMEM] + [pl.BlockSpec((1, 512, 512), lambda i: (layer, 0, 0))] * 2,
        out_specs=VMEM,
        compiler_params=PARAMS,
        cost_estimate=pl.CostEstimate(flops=2 * 256 * 512 * 1024, bytes_accessed=2_000_000, transcendentals=0),
    )(mixed, near, far)


def sum_kernel(recv_ref, held_ref, out_ref, own_ref):
    total = held_ref[...].astype(f32)
    for d in range(GRID):
        total = total + recv_ref[d].astype(f32)
    own = total.astype(bf16)
    own_ref[...] = own
    for d in range(GRID):
        out_ref[d] = own


def weigh_kernel(query_ref, pair_ref, gain_ref, out_ref):
    rows = lax.broadcasted_iota(jnp.int32, (256, 256), 0)
    cols = lax.broadcasted_iota(jnp.int32, (256, 256), 1)
    scale = jnp.sum(jnp.where(rows == cols, gain_ref[...], 0.0), axis=1, keepdims=True)
    pair = (pair_ref[0].astype(f32) * scale).astype(bf16)
    for d in range(4):
        query = query_ref[0, :, 512 * d : 512 * (d + 1)]
        out_ref[d, :, :512] = (query.astype(f32) * scale).astype(bf16)
        out_ref[d, :, 512:] = pair[:, 256 * (d // 2) : 256 * (d // 2 + 1)]


def weigh(w_query, w_pair, gain):
    return pl.pallas_call(
        weigh_kernel,
        out_shape=jax.ShapeDtypeStruct((4, 512, 768), bf16),
        grid=(2,),
        in_specs=[
            pl.BlockSpec((1, 256, 2048), lambda i: (0, i, 0)),
            pl.BlockSpec((1, 256, 512), lambda i: (0, i, 0)),
            pl.BlockSpec((1, 256), lambda i: (0, i)),
        ],
        out_specs=pl.BlockSpec((4, 256, 768), lambda i: (0, i, 0)),
        compiler_params=STREAM,
        cost_estimate=pl.CostEstimate(flops=2_000_000, bytes_accessed=6_000_000, transcendentals=0),
    )(w_query, w_pair, gain)


def choose(arrays, is_index):
    chosen = arrays[0]
    for i in range(1, len(arrays)):
        chosen = jnp.where(is_index[i], arrays[i], chosen)
    return chosen


def traded(value, bits):
    return lax.ppermute(value, "section", [(s, s ^ bits) for s in range(4)])


def segment_info(lengths_row, total):
    token_ids = jnp.arange(total, dtype=jnp.int32)
    ends = jnp.cumsum(lengths_row)
    after = (token_ids[:, None] >= ends[None, :]).astype(jnp.int32)
    seg_ids = jnp.sum(after, axis=1)
    starts = jnp.sum(after * lengths_row[None, :], axis=1)
    return (seg_ids, token_ids - starts)


def swap(value):
    return lax.ppermute(value, "core", [(0, 1), (1, 0)])


def exchange(value, axis):
    return lax.all_to_all(value, axis, 0, 0, tiled=True)


def local(hidden_in, lengths, gain, w_query, w_pair, w_out):
    section = lax.axis_index("section")
    place = lax.axis_index("z")
    core = lax.axis_index("core")
    grid_place = section * 4 + lax.axis_index("row")

    near_in = exchange(weigh(w_query, w_pair, gain), "section")
    blocks_out = [lax.dynamic_slice(w_out, (0, 512 * (section ^ k), 0), (1, 512, 512))[0] for k in range(4)]
    turn = [section ^ layer for layer in range(LAYERS)]

    mine = lax.dynamic_index_in_dim(hidden_in, core, 0, keepdims=False)
    theirs = lax.dynamic_index_in_dim(hidden_in, 1 - core, 0, keepdims=False)
    x = jnp.concatenate([mine, swap(theirs)], axis=1)
    held = lax.dynamic_slice_in_dim(x, grid_place * PART, PART, 0)

    seg, pos = segment_info(lax.dynamic_index_in_dim(lengths, core, 0, keepdims=False), TOK)
    seg_window = lax.dynamic_slice_in_dim(jnp.pad(seg, (HALO, 0), constant_values=-1), place * OWN, WINDOW)
    pos_window = lax.dynamic_slice_in_dim(jnp.pad(pos, (HALO, 0)), place * OWN, WINDOW)
    exponent = jnp.arange(HEAD // 2, dtype=f32) * (2.0 / HEAD)
    freqs = jnp.power(f32(ROPE_BASE), -exponent)
    angles = pos_window.astype(f32)[:, None] * freqs[None, :]
    cosine = jnp.cos(angles)
    sine = jnp.sin(angles)
    cosine = jnp.concatenate([cosine, cosine], axis=1)
    sine = jnp.concatenate([-sine, sine], axis=1)
    allowed = (seg_window[HALO:, None] == seg_window[None, :]) & (pos_window[None, :] <= pos_window[HALO:, None])
    mask = allowed.astype(f32)
    place_arg = place.reshape(1).astype(jnp.int32)

    def attend(recv):
        return pl.pallas_call(
            attend_kernel,
            out_shape=jax.ShapeDtypeStruct((CHIPS, OWN, 512), bf16),
            in_specs=[pl.BlockSpec(memory_space=pltpu.SMEM)] + [VMEM] * 4,
            out_specs=VMEM,
            compiler_params=PARAMS,
            cost_estimate=pl.CostEstimate(flops=10_000_000, bytes_accessed=1_000_000, transcendentals=20_000),
        )(place_arg, recv, cosine, sine, mask)

    is_section = [(section == layer).astype(jnp.int32).reshape(1) for layer in range(LAYERS)]
    is_turn = [[turn[layer] == k for k in range(4)] for layer in range(LAYERS)]
    is_first = lengths[0, 0] > 0
    is_last = section == LAYERS - 1
    is_core = core == 0
    near_in, x, held, cosine, sine, mask, place_arg, is_first, is_last, is_core, is_section, is_turn, blocks_out = (
        lax.optimization_barrier(
            (near_in, x, held, cosine, sine, mask, place_arg, is_first, is_last, is_core, is_section, is_turn, blocks_out)
        )
    )
    def mix(packed):
        return attend(exchange(packed, "z"))

    def begin(x, near_in, far_first):
        (packed,) = project(x, near_in, far_first, 0, 0, None, None)
        return mix(packed)

    far_first = swap(near_in[:1])
    moved_out = [blocks_out[0]] + [traded(blocks_out[k], k) for k in range(1, 4)]
    kept = None
    for layer in range(LAYERS):
        if layer == 1:
            (packed,) = project(x, near_in, far_in, layer, layer, None, None)
            kept = x
        elif layer > 1:
            packed, kept = project(x, near_in, far_in, layer, layer, kept, is_section[layer - 1])
        if layer == 0:
            copies = lax.cond(is_first, begin, lambda *_: jnp.zeros((CHIPS, OWN, 512), bf16), x, near_in, far_first)
            copies, moved_out, rest = lax.optimization_barrier((copies, moved_out, near_in))
            near_out = jnp.stack([choose(moved_out, is_turn[each]) for each in range(LAYERS)])
            copies, near_out = lax.optimization_barrier((copies, near_out))
            far_out = swap(near_out)
            far_in = swap(rest)
        else:
            copies = mix(packed)
        mixed = exchange(copies, "z").reshape(TOK, 512)
        branch = spread(mixed, near_out, far_out, layer)
        copies, held = call(
            sum_kernel,
            (jax.ShapeDtypeStruct((GRID, PART, 1024), bf16), jax.ShapeDtypeStruct((PART, 1024), bf16)),
            (exchange(branch.reshape(GRID, PART, 1024), ("section", "row")), held),
            256 * 1024,
        )
        x = exchange(copies, ("section", "row")).reshape(TOK, 1024)

    kept = jnp.where(is_last, x, kept)
    ours = kept[:, :512]
    other = swap(kept[:, 512:])
    final = jnp.where(is_core, jnp.stack([ours, other]), jnp.stack([other, ours]))
    return final[None]


def solution(mesh):
    split = Mesh(mesh.devices.reshape(4, 4, 8, 2), ("section", "row", "z", "core"))
    col = ("z", "core")
    in_specs = (
        P(None, None, col),
        P(),
        P("section", col),
        P("section", col, "row"),
        P("section", col, "row"),
        P("section", "row", col),
    )
    out_specs = P("section", None, None, col)
    return jax.shard_map(local, mesh=split, in_specs=in_specs, out_specs=out_specs, check_vma=False)
```
